256 devices in a mesh: batch: 16 (over z, core), vocab: 16 (over x, y).
Axes of the slice: x: 4, y: 4, z: 8, core: 2. Of those that a mesh axis runs over, the one named last changes fastest.
Arguments:
- queries: bfloat16 [256, 8192], P('batch'), may hold values from -6 to 8
- key_new: bfloat16 [256, 1024], P('batch'), may hold values from -6 to 6
- value_new: bfloat16 [256, 1024], P('batch'), may hold values from -6 to 6
- key_cache: bfloat16 [256, 256, 1024], P('batch', 'vocab'), may hold values from -6 to 6
- value_cache: bfloat16 [256, 256, 1024], P('batch', 'vocab'), may hold values from -6 to 6
- parents: int32 [256], replicated, may hold values from 0 to 255, as said below
- tokens: int32 [256], replicated, may hold values from 0 to 128255
- hidden: bfloat16 [256, 8192], P(None, 'batch'), may hold values from -40 to 40
- out_weight: bfloat16 [8192, 8192], P('vocab', 'batch'), may hold values from -4.5 to 4.5
- final_gain: float32 [8192], P('batch'), may hold values from 0.5 to 1.5
- head_weight: bfloat16 [128256, 8192], P(('batch', 'vocab')), may hold values from -3.25 to 3.25
- past_scores: float32 [256, 128256], P(None, ('batch', 'vocab')), may hold values from -3 to -0.5
Outputs:
- next_keys: bfloat16 [256, 256, 1024], P('batch', 'vocab')
- next_values: bfloat16 [256, 256, 1024], P('batch', 'vocab')
- candidates: float32 [256, 128256], P(None, ('batch', 'vocab'))
The draws below stay inside these ranges and needn't reach their ends.
Inputs may be any that keep to these rules, and one draw needn't show every extreme that they name: Hypothesis i, in block b = i // 16 at row r = i % 16, is beam b // 2 of request ((b % 2 - b // 2) mod 2) * 16 + r, and parents[i] is a hypothesis of the same request. Within each aligned block of 16 hypotheses, at most 4 have their parents in any one aligned block of 16 hypotheses, and every block reaches 4.
All inputs are finite; a program needn't handle non-finite values.
Results may differ from the reference program's by a relative error of at most 0.0052.
Values may be sent and summed in bfloat16 or wider, within the bound.
A program may use at most 128 MiB of HBM per device.

```python
import jax
import jax.numpy as jnp
from jax import lax

D = 8192
HEADS = 64
KV_HEADS = 8
HEAD_DIM = 128
VOCAB = 128256
BEAMS = 8
HYP_DEV = 16
POS = 256
HYP = 256
CLASSES = 2
CAP = 4


def draw_queries(key, part):
    key = jax.random.fold_in(key, 3)
    array_shape = (HYP, HEADS * HEAD_DIM)
    values = jax.random.normal(key, array_shape, jnp.float32)
    return jnp.clip(values, -6.0, 8.0).astype(jnp.bfloat16)


def draw_key_cache(key, part):
    key = jax.random.fold_in(key, 5)
    array_shape = (HYP, POS, KV_HEADS * HEAD_DIM)
    fraction = (jnp.arange(POS, dtype=jnp.float32) / POS)[None, :, None]
    values = 0.4 * 6.0 ** fraction * jax.random.normal(key, array_shape, jnp.float32)
    return jnp.clip(values, -6.0, 6.0).astype(jnp.bfloat16)


def draw_parents(key, part):
    key = jax.random.fold_in(key, 11)

    def one_block(block_key):
        first_key, second_key, third_key = jax.random.split(block_key, 3)
        favored = jax.random.randint(first_key, (), 0, BEAMS)
        ordering = jax.random.permutation(second_key, (BEAMS - 1) * CAP)
        others = (favored + 1 + ordering[:HYP_DEV - CAP] // CAP) % BEAMS
        chosen = jnp.concatenate([jnp.full((CAP,), favored, jnp.int32), others.astype(jnp.int32)])
        return jax.random.permutation(third_key, chosen)
    block_count = HYP // HYP_DEV
    parent_beams = jax.vmap(one_block)(jax.random.split(key, block_count)).astype(jnp.int32)
    block_ids = jnp.arange(block_count, dtype=jnp.int32)
    request_class = (block_ids % CLASSES - block_ids // CLASSES) % CLASSES
    parent_block = parent_beams * CLASSES + (request_class[:, None] + parent_beams) % CLASSES
    row_ids = jnp.arange(HYP_DEV, dtype=jnp.int32)[None, :]
    return (parent_block * HYP_DEV + row_ids).reshape(HYP).astype(jnp.int32)


def draw_hidden(key, part):
    key = jax.random.fold_in(key, 7)
    first_key = jax.random.fold_in(key, 0)
    second_key = jax.random.fold_in(key, 1)
    fourth_key = jax.random.fold_in(key, 3)
    column = jnp.arange(D, dtype=jnp.float32) / D
    row_scale = 10.0 ** jax.random.uniform(first_key, (HYP, 1), jnp.float32, -0.5, 0.5)
    column_scale = jnp.exp(jax.random.uniform(second_key, (D,), jnp.float32, -1.15, 1.15))
    rising = 8.0 ** column
    values = 0.15 * rising * column_scale * row_scale * jax.random.normal(fourth_key, (HYP, D), jnp.float32)
    return jnp.clip(values, -40.0, 40.0).astype(jnp.bfloat16)


def draw_out_weight(key, part):
    key = jax.random.fold_in(key, 13)
    array_shape = (HEADS * HEAD_DIM, D)
    column = (jnp.arange(D, dtype=jnp.float32) / D)[None, :]
    base_scale = HEAD_DIM ** (-0.5)
    values = 8.0 ** column * base_scale * jax.random.normal(key, array_shape, jnp.float32)
    return jnp.clip(values, -4.5, 4.5).astype(jnp.bfloat16)


def draw_head_weight(key, part):
    key = jax.random.fold_in(key, 9)
    first_key = jax.random.fold_in(key, 0)
    array_shape = (VOCAB, D)
    spread_scale = 3.0 * D ** (-0.5)
    row_fraction = (jnp.arange(VOCAB, dtype=jnp.float32) / VOCAB)[:, None]
    row_scale = 0.5 * 3.0 ** row_fraction
    values = jax.random.normal(first_key, array_shape, jnp.float32) * spread_scale * row_scale
    return jnp.clip(values, -3.25, 3.25).astype(jnp.bfloat16)


def with_ends(drawn, own_key, least, high):
    place = [jax.random.randint(jax.random.fold_in(own_key, axis), (), 0, length) for axis, length in enumerate(drawn.shape)]
    main_axis = drawn.shape.index(max(drawn.shape))
    neighbour = place[:main_axis] + [(place[main_axis] + 1) % drawn.shape[main_axis]] + place[main_axis + 1:]
    return drawn.at[tuple(place)].set(least).at[tuple(neighbour)].set(high)


def block_levels(stream_key, dims, pieces, low, high):
    gain, own = 1.0, jax.random.fold_in(stream_key, 6)
    for axis_at, blocks in pieces:
        steps = jnp.exp(jax.random.uniform(jax.random.fold_in(own, axis_at), (blocks,), jnp.float32, low / len(pieces), high / len(pieces)))
        gain = gain * jnp.repeat(steps, dims[axis_at] // blocks).reshape([-1 if axis == axis_at else 1 for axis in range(len(dims))])
    return gain


def normal_values(key, extent, width, limit, cuts=(), held_as=jnp.bfloat16):
    result = width * jax.random.normal(key, extent, jnp.float32)
    if cuts:
        result = result * block_levels(key, extent, cuts, -0.22, 0.18)
    return jnp.clip(result, -limit, limit).astype(held_as)


def setup_inputs(seed: int = 0) -> dict:
    keys = jax.random.split(jax.random.key(seed), 13)
    return {
        "queries": draw_queries(jax.random.fold_in(keys[12], 71), 0),
        "key_new": normal_values(keys[1], (HYP, KV_HEADS * HEAD_DIM), 1.0, 6.0, ((0, 16),)),
        "value_new": normal_values(keys[2], (HYP, KV_HEADS * HEAD_DIM), 1.0, 6.0, ((0, 16),)),
        "key_cache": draw_key_cache(jax.random.fold_in(keys[12], 71), 0),
        "value_cache": normal_values(keys[4], (HYP, POS, KV_HEADS * HEAD_DIM), 1.0, 6.0, ((0, 16), (1, 16))),
        "parents": draw_parents(jax.random.fold_in(keys[12], 71), 0),
        "tokens": with_ends(jax.random.randint(keys[6], (HYP,), 0, VOCAB), jax.random.fold_in(keys[6], 1), 0, VOCAB - 1).astype(jnp.int32),
        "hidden": draw_hidden(jax.random.fold_in(keys[12], 71), 0),
        "out_weight": draw_out_weight(jax.random.fold_in(keys[12], 71), 0),
        "final_gain": jnp.clip(1.0 + 0.1 * jax.random.normal(keys[9], (D,), jnp.float32), 0.5, 1.5),
        "head_weight": draw_head_weight(jax.random.fold_in(keys[12], 71), 0),
        "past_scores": jnp.clip(-3.0 + 2.5 * jax.random.uniform(keys[11], (HYP, VOCAB), jnp.float32) ** block_levels(keys[11], (HYP, VOCAB), ((1, 256),), -0.2, 0.2), -3.0, -0.5),
    }


def reference(queries, key_new, value_new, key_cache, value_cache, parents, tokens, hidden, out_weight, final_gain, head_weight, past_scores):
    group_size = HEADS // KV_HEADS
    next_keys = jnp.take(key_cache, parents, axis=0).at[:, POS - 1, :].set(key_new)
    next_values = jnp.take(value_cache, parents, axis=0).at[:, POS - 1, :].set(value_new)
    query_groups = queries.reshape(HYP, KV_HEADS, HEAD_DIM, group_size).astype(jnp.float32)
    key_groups = next_keys.reshape(HYP, POS, KV_HEADS, HEAD_DIM).astype(jnp.float32)
    scores = jnp.einsum('nhde,nphd->nhep', query_groups, key_groups) * HEAD_DIM ** (-0.5)
    highest = lax.optimization_barrier(jnp.max(scores, axis=3, keepdims=True))
    weights = jnp.exp(scores - highest)
    rounded = (weights / lax.optimization_barrier(jnp.sum(weights, axis=3, keepdims=True))).astype(jnp.bfloat16)
    value_groups = next_values.reshape(HYP, POS, KV_HEADS, HEAD_DIM).astype(jnp.float32)
    mixture = jnp.einsum('nhep,nphd->nhde', rounded.astype(jnp.float32), value_groups)
    attended = mixture.reshape(HYP, HEADS * HEAD_DIM).astype(jnp.bfloat16)
    residual = hidden.astype(jnp.float32) + jnp.dot(attended, out_weight, preferred_element_type=jnp.float32)
    squares = lax.optimization_barrier(jnp.sum(residual * residual, axis=1, keepdims=True))
    normed = (residual * lax.rsqrt(squares / D + 1e-05) * final_gain).astype(jnp.bfloat16)
    logits = lax.dot_general(normed, head_weight, (((1,), (1,)), ((), ())), preferred_element_type=jnp.float32)
    largest = lax.optimization_barrier(jnp.max(logits, axis=1))
    log_total = largest + jnp.log(lax.optimization_barrier(jnp.sum(jnp.exp(logits - largest[:, None]), axis=1)))
    beam_score = past_scores[parents, tokens]
    candidates = beam_score[:, None] + (logits - log_total[:, None])
    return (next_keys, next_values, candidates)
```

```python
import functools

import jax
import jax.numpy as jnp
from jax import lax
from jax.experimental import pallas as pl
from jax.experimental.pallas import tpu as pltpu
from jax.sharding import PartitionSpec as P

D = 8192
HEAD_DIM = 128
MESH = pl.DeviceIdType.MESH
F32 = jnp.float32
BF16 = jnp.bfloat16
NT = (((1,), (1,)), ((), ()))

BULK_EARLY_K = (1, 7, 2, 6, 4)
BULK_EARLY_V = ()
BULK_LATE_K = (3, 5)
BULK_LATE_V = (1, 7, 2, 6, 3, 5, 4)


def iota(shape, axis):
    return lax.broadcasted_iota(jnp.int32, shape, axis)


def kernel(
    q_ref, kn_ref, vn_ref, kc_ref, vc_ref, par_ref, tok_ref, hid_ref, w_ref, gain_ref, hw_ref, past_ref,
    nk_ref, nv_ref, cand_ref,
    q_v, kn_v, vn_v, kc_v, vc_v, hid_v, w_v, hw_v, past_v,
    kt, vt, xs, xr, perm, qp, kn_s, vn_s, o_s, rs, ar, a_s, aa, ps, pr,
    ks, vs, kr, vr, nb, sq_s, sq_r, sc_s, sc_r, acc, pick, lv_s, lv_r, lb_s, lb_r,
    lsem, rsem, ssem, s1, s2, t1, t2,
):
    b = lax.axis_index("batch")
    v = lax.axis_index("vocab")
    z, c = b // 2, b % 2
    kind = (c + z) % 2
    g, h = v // 2, v % 2
    x, y = v // 4, v % 4

    def same_kind(zz):
        return 2 * zz + (kind + zz) % 2

    def send(src, dst, send_sem, recv_sem, dev):
        pltpu.make_async_remote_copy(
            src_ref=src, dst_ref=dst, send_sem=send_sem, recv_sem=recv_sem,
            device_id=dev, device_id_type=MESH,
        ).start()

    def wait(ref, sem):
        pltpu.make_async_copy(ref, ref, sem).wait()

    local = [
        pltpu.make_async_copy(q_ref.at[:, pl.ds(pl.multiple_of(g * 1024, 1024), 1024)], q_v, lsem.at[0]),
        pltpu.make_async_copy(kn_ref, kn_v, lsem.at[1]),
        pltpu.make_async_copy(vn_ref, vn_v, lsem.at[2]),
        pltpu.make_async_copy(kc_ref, kc_v, lsem.at[3]),
        pltpu.make_async_copy(vc_ref, vc_v, lsem.at[4]),
        pltpu.make_async_copy(past_ref, past_v, lsem.at[5]),
        pltpu.make_async_copy(w_ref, w_v, lsem.at[6]),
        pltpu.make_async_copy(hid_ref.at[pl.ds(pl.multiple_of(v * 16, 16), 16)], hid_v, lsem.at[7]),
        pltpu.make_async_copy(hw_ref, hw_v, lsem.at[8]),
    ]
    for copy in local:
        copy.start()

    bar = pltpu.get_barrier_semaphore()

    def greet(d, _):
        pl.semaphore_signal(bar, inc=1, device_id=(b, (v + d) % 16), device_id_type=MESH)
        pl.semaphore_signal(bar, inc=1, device_id=((b + d) % 16, v), device_id_type=MESH)
        pl.semaphore_signal(bar, inc=1, device_id=((b + d) % 16, 2 * g + 1 - h), device_id_type=MESH)
        return 0

    lax.fori_loop(1, 16, greet, 0)

    for copy in local[:3]:
        copy.wait()
    lane_g = pl.ds(pl.multiple_of(g * 128, 128), 128)
    packed = jnp.concatenate(
        [q_v[...].astype(F32), kn_v[:, lane_g].astype(F32), vn_v[:, lane_g].astype(F32)], axis=1
    )
    upper = h.astype(F32)
    packed = packed[0:8] * (1.0 - upper) + packed[8:16] * upper
    packed = jnp.concatenate([packed[:, :640], packed[:, 640:]], axis=0).astype(BF16)
    xs[...] = packed
    xr[z] = packed

    pl.semaphore_wait(bar, 45)

    def send_query(d, _):
        zz = (z + d) % 8
        send(xs, xr.at[z], ssem.at[0], rsem.at[0], (same_kind(zz), v))
        return 0

    lax.fori_loop(1, 8, send_query, 0)

    def cache_part(ref, target):
        rows = pl.ds(pl.multiple_of((target % 2) * 8, 8), 8)
        return ref.at[rows, :, pl.ds(pl.multiple_of((target // 2) * 128, 128), 128)]

    my_pos = pl.ds(pl.multiple_of(v * 16, 16), 16)

    def turn(ref, out, i):
        def step(d, _):
            t = (v + d) % 16
            send(cache_part(ref, t), out.at[:, my_pos, :], ssem.at[i], rsem.at[i], (b, t))
            return 0

        lax.fori_loop(1, 16, step, 0)
        pltpu.make_async_copy(cache_part(ref, v), out.at[:, my_pos, :], rsem.at[i]).start()

    turn(kc_ref, kt, 1)
    turn(vc_ref, vt, 2)

    local[3].wait()
    local[4].wait()

    def stage(zz, _):
        base = same_kind(zz) * 16
        count = jnp.int32(0)
        rows = [jnp.int32(0)] * 4
        for r in range(16):
            mine = (par_ref[base + r] // 32 == z).astype(jnp.int32)
            for k in range(4):
                rows[k] = jnp.where(count * mine + mine == k + 1, r, rows[k])
            count = count + mine
        for k in range(4):
            ks[zz, k] = kc_v[rows[k]]
            vs[zz, k] = vc_v[rows[k]]
        return 0

    lax.fori_loop(0, 8, stage, 0)
    kr[z] = ks[z]
    vr[z] = vs[z]

    def bulk(src, dst, i, distances):
        for d in distances:
            zz = (z + d) % 8
            send(src.at[zz], dst.at[z], ssem.at[i], rsem.at[i], (same_kind(zz), v))

    bulk(ks, kr, 3, BULK_EARLY_K)
    bulk(vs, vr, 4, BULK_EARLY_V)

    lanes = iota((128, 1024), 1)
    wanted = (lanes % 128) * 8 + lanes // 128
    subs = iota((128, 1024), 0)

    def build(t, _):
        perm[pl.ds(pl.multiple_of(t * 128, 128), 128), :] = (subs + t * 128 == wanted).astype(F32).astype(BF16)
        return 0

    lax.fori_loop(0, 8, build, 0)
    k64 = iota((64, 64), 0)
    swap = (iota((64, 64), 1) == (k64 % 8) * 8 + k64 // 8).astype(F32).astype(BF16)

    local[5].wait()
    first_token = (b * 16 + v) * 501
    lane501 = iota((1, 501), 1)

    def pick_row(i, _):
        row = past_v[pl.ds(par_ref[i], 1), :]
        hit = jnp.where(lane501 == tok_ref[i] - first_token, row, 0.0)
        pick[pl.ds(i, 1), :] = jnp.sum(hit, axis=1, keepdims=True)
        return 0

    lax.fori_loop(0, 256, pick_row, 0)

    wait(xr.at[0:7], rsem.at[0])
    got = xr[...].astype(F32)
    got = jnp.concatenate(
        [got[:, 0:8, :].reshape(64, 640), got[:, 8:16, :].reshape(64, 640)], axis=1
    ).astype(BF16)
    got = jnp.dot(swap, got, preferred_element_type=F32)
    kn_s[...] = got[:, 1024:1152]
    vn_s[...] = got[:, 1152:1280]
    qp[...] = jnp.dot(got[:, :1024].astype(BF16), perm[...], preferred_element_type=F32)
    wait(kt, rsem.at[1])
    wait(vt, rsem.at[2])
    lane256 = iota((64, 256), 1)

    def attend(r, _):
        rows = pl.ds(pl.multiple_of(r * 8, 8), 8)
        qr = qp[rows, :]
        qf = jnp.concatenate([qr[:, j * 128:(j + 1) * 128] for j in range(8)], axis=0)
        new_key = jnp.concatenate([kn_s[rows, :]] * 8, axis=0)
        new_value = jnp.concatenate([vn_s[rows, :]] * 8, axis=0)
        s = lax.dot_general(qf.astype(BF16), kt[r], NT, preferred_element_type=F32)
        s_new = jnp.sum(qf * new_key, axis=1, keepdims=True)
        s = jnp.where(lane256 == 255, s_new, s) * HEAD_DIM ** (-0.5)
        e = jnp.exp(s - jnp.max(s, axis=1, keepdims=True))
        wf = (e / jnp.sum(e, axis=1, keepdims=True)).astype(BF16).astype(F32)
        w_new = wf[:, 255:256]
        w_old = jnp.where(lane256 == 255, 0.0, wf).astype(BF16)
        o = jnp.dot(w_old, vt[r], preferred_element_type=F32) + w_new * new_value
        o_s[rows, :] = jnp.concatenate([o[j * 8:(j + 1) * 8] for j in range(8)], axis=1)
        return 0

    lax.fori_loop(0, 8, attend, 0)
    o = lax.dot_general(o_s[...].astype(BF16), perm[...], NT, preferred_element_type=F32).astype(BF16)
    o = jnp.dot(swap, o, preferred_element_type=F32).reshape(8, 8, 1024)
    rs[...] = jnp.concatenate([o[:, :, :512], o[:, :, 512:]], axis=1).astype(BF16)
    ar[z] = rs[z]

    def send_back(d, _):
        zz = (z + d) % 8
        send(rs.at[zz], ar.at[z], ssem.at[5], rsem.at[5], (same_kind(zz), v))
        return 0

    lax.fori_loop(1, 8, send_back, 0)
    sub16 = iota((16, 512), 0)
    beam = jnp.zeros((16, 512), jnp.int32)
    for r in range(8):
        beam = jnp.where(sub16 % 8 == r, par_ref[b * 16 + h * 8 + r] // 32, beam)
    wait(ar.at[0:7], rsem.at[5])
    att = jnp.zeros((16, 512), F32)
    for p in range(8):
        att = jnp.where(beam == p, ar[p].astype(F32), att)
    for hh in range(2):
        part = att[hh * 8:hh * 8 + 8]
        a_s[hh] = jnp.concatenate([part[:, :256], part[:, 256:]], axis=0).astype(BF16)
    aa[2 * b + h] = a_s[h]

    slot = aa.at[2 * b + h]
    send(a_s.at[1 - h], slot, ssem.at[6], rsem.at[6], (b, 2 * g + 1 - h))

    def spread(d, _):
        for hh in range(2):
            send(a_s.at[hh], slot, ssem.at[6], rsem.at[6], ((b + d) % 16, 2 * g + hh))
        return 0

    lax.fori_loop(1, 16, spread, 0)
    local[6].wait()
    local[7].wait()
    wait(aa.at[0:31], rsem.at[6])
    rows_in = aa[...].astype(F32)
    rows_in = jnp.concatenate(
        [rows_in[:, 0:8, :].reshape(256, 256), rows_in[:, 8:16, :].reshape(256, 256)], axis=1
    ).astype(BF16)
    ps[...] = jnp.dot(rows_in, w_v[...], preferred_element_type=F32).astype(BF16).reshape(16, 16, 512)
    pr[v] = ps[v]

    def send_partial(d, _):
        t = (v + d) % 16
        send(ps.at[t], pr.at[v], ssem.at[7], rsem.at[7], (b, t))
        return 0

    lax.fori_loop(1, 16, send_partial, 0)
    wait(pr.at[0:15], rsem.at[7])
    residual = hid_v[...].astype(F32) + jnp.sum(pr[...].astype(F32), axis=0)
    nb[c, v, z] = (residual * gain_ref[...]).astype(BF16)

    def send_state(d, _):
        zz = (z + d) % 8
        send(nb.at[c, v, z], nb.at[c, v, z], ssem.at[8], rsem.at[8], (2 * zz + c, v))
        return 0

    lax.fori_loop(1, 8, send_state, 0)
    diag16 = iota((16, 128), 0) == iota((16, 128), 1)
    square = jnp.sum(residual * residual, axis=1, keepdims=True)
    square = jnp.sum(jnp.where(diag16, square, 0.0), axis=0, keepdims=True)
    sq_s[...] = square
    sq_r[b] = square

    def send_square(d, _):
        send(sq_s, sq_r.at[b], ssem.at[9], rsem.at[9], ((b + d) % 16, v))
        return 0

    lax.fori_loop(1, 16, send_square, 0)
    wait(nb.at[0, 0, 0:7], rsem.at[8])

    def along(u, axis, d):
        if axis == 0:
            return ((u // 4 + d) % 4) * 4 + u % 4
        return (u // 4) * 4 + (u % 4 + d) % 4

    def piece(u, half, part=None):
        if part is None:
            return nb.at[c, u, 4 * half:4 * half + 4]
        return nb.at[c, u, 4 * half + 2 * part:4 * half + 2 * part + 2]

    def state(ref, axis, d, sem):
        send(ref, ref, ssem.at[10], sem, (b, along(v, axis, d)))

    def sibling(ref):
        send(ref, ref, ssem.at[11], rsem.at[10], (2 * z + 1 - c, v))

    halves = ((1, 0), (0, 1))

    def first(half, order=halves):
        axis = order[half][0]
        state(piece(v, half), axis, 1, s1.at[half, 0])
        state(piece(v, half), axis, -1, s1.at[half, 1])

    def second(half, o):
        u = along(v, halves[half][0], o)
        axis = halves[half][1]
        state(piece(u, half), axis, 1, t1.at[half, o, 0])
        state(piece(u, half), axis, -1, t1.at[half, o, 1])

    def second_forward(half, o):
        u = along(v, halves[half][0], o)
        axis = halves[half][1]
        wait(piece(u, half), t1.at[half, o, 0])
        state(piece(along(u, axis, -1), half, 0), axis, 1, t2.at[half, o, 0])
        sibling(piece(along(u, axis, -1), half))
        wait(piece(u, half), t1.at[half, o, 1])
        state(piece(along(u, axis, 1), half, 1), axis, -1, t2.at[half, o, 1])
        sibling(piece(along(u, axis, 1), half))

    for half in range(2):
        first(half)
    for half in range(2):
        second(half, 0)
        sibling(piece(v, half))
    for half in range(2):
        axis = halves[half][0]
        wait(piece(v, half), s1.at[half, 0])
        state(piece(along(v, axis, -1), half, 0), axis, 1, s2.at[half, 0])
        wait(piece(v, half), s1.at[half, 1])
        state(piece(along(v, axis, 1), half, 1), axis, -1, s2.at[half, 1])
    for half in range(2):
        second(half, 3)
        second(half, 1)
        sibling(piece(along(v, halves[half][0], -1), half))
        sibling(piece(along(v, halves[half][0], 1), half))
    bulk(ks, kr, 3, BULK_LATE_K)
    bulk(vs, vr, 4, BULK_LATE_V)
    for half in range(2):
        second_forward(half, 0)
    for half in range(2):
        wait(piece(v, half, 0), s2.at[half, 0])
        wait(piece(v, half, 1), s2.at[half, 1])
        second(half, 2)
        sibling(piece(along(v, halves[half][0], 2), half))

    wait(sq_r.at[0:15], rsem.at[9])
    scale = lax.rsqrt(jnp.sum(sq_r[...], axis=0) / D + 1e-05)
    sc_s[...] = scale
    sc_r[v] = scale

    def send_scale(d, _):
        send(sc_s, sc_r.at[v], ssem.at[12], rsem.at[11], (b, (v + d) % 16))
        return 0

    lax.fori_loop(1, 16, send_scale, 0)
    for o in (3, 1, 2):
        for half in range(2):
            second_forward(half, o)
    for o in (0, 3, 1, 2):
        for half in range(2):
            u = along(v, halves[half][0], o)
            axis = halves[half][1]
            wait(piece(u, half, 0), t2.at[half, o, 0])
            wait(piece(u, half, 1), t2.at[half, o, 1])
            sibling(piece(along(u, axis, 2), half))

    local[8].wait()

    def product(core, zz):
        cols = pl.ds(pl.multiple_of((2 * zz + core) * 512, 512), 512)
        return lax.dot_general(
            nb[core, :, zz].reshape(256, 512), hw_v[:, cols], NT, preferred_element_type=F32
        )

    acc[...] = product(c, 0)

    def own_share(zz, _):
        acc[...] += product(c, zz)
        return 0

    lax.fori_loop(1, 8, own_share, 0)
    wait(nb.at[0], rsem.at[10])

    def other_share(zz, _):
        acc[...] += product(1 - c, zz)
        return 0

    lax.fori_loop(0, 8, other_share, 0)
    wait(sc_r.at[0:15], rsem.at[11])
    diag3 = iota((16, 16, 128), 1) == iota((16, 16, 128), 2)
    scales = jnp.sum(jnp.where(diag3, sc_r[...], 0.0), axis=2, keepdims=True).reshape(256, 1)
    logits = acc[...] * scales
    acc[...] = logits
    largest = jnp.max(logits, axis=1, keepdims=True)
    total = jnp.sum(jnp.exp(logits - largest), axis=1, keepdims=True)
    diag128 = iota((128, 128), 0) == iota((128, 128), 1)

    def to_rows(column):
        parts = [
            jnp.sum(jnp.where(diag128, column[k * 128:(k + 1) * 128], 0.0), axis=0, keepdims=True)
            for k in range(2)
        ]
        return jnp.concatenate(parts, axis=0)

    def to_column(rows):
        parts = [
            jnp.sum(jnp.where(diag128, rows[k:k + 1], 0.0), axis=1, keepdims=True) for k in range(2)
        ]
        return jnp.concatenate(parts, axis=0)

    def merged(stats):
        high = jnp.max(stats[:, 0:2], axis=0)
        return jnp.concatenate(
            [
                high,
                jnp.sum(stats[:, 2:4] * jnp.exp(stats[:, 0:2] - high), axis=0),
                jnp.sum(stats[:, 4:6], axis=0),
                jnp.zeros((2, 128), F32),
            ],
            axis=0,
        )

    stats = jnp.concatenate(
        [to_rows(largest), to_rows(total), to_rows(pick[...]), jnp.zeros((2, 128), F32)], axis=0
    )
    lv_s[...] = stats
    lv_r[v] = stats

    def send_vocab(d, _):
        send(lv_s, lv_r.at[v], ssem.at[13], rsem.at[12], (b, (v + d) % 16))
        return 0

    lax.fori_loop(1, 16, send_vocab, 0)
    wait(lv_r.at[0:15], rsem.at[12])
    stats = merged(lv_r[...])
    lb_s[...] = stats
    lb_r[b] = stats

    def send_batch(d, _):
        send(lb_s, lb_r.at[b], ssem.at[14], rsem.at[13], ((b + d) % 16, v))
        return 0

    lax.fori_loop(1, 16, send_batch, 0)

    wait(kr.at[0:7], rsem.at[3])
    wait(vr.at[0:7], rsem.at[4])
    last = iota((16, 1024), 0) == jnp.where(v == 15, 15, 99)
    new_keys = kn_v[...].astype(F32)
    new_values = vn_v[...].astype(F32)
    beams = [par_ref[b * 16 + r] // 32 for r in range(16)]
    for r in range(16):
        at = jnp.int32(0)
        for earlier in range(r):
            at = at + (beams[earlier] == beams[r]).astype(jnp.int32)
        at = jnp.minimum(at, 3)
        nk_ref[r] = jnp.where(last, new_keys[r:r + 1], kr[beams[r], at].astype(F32)).astype(BF16)
        nv_ref[r] = jnp.where(last, new_values[r:r + 1], vr[beams[r], at].astype(F32)).astype(BF16)

    wait(lb_r.at[0:15], rsem.at[13])
    stats = merged(lb_r[...])
    offset = stats[4:6] - (stats[0:2] + jnp.log(stats[2:4]))
    cand_ref[...] = acc[...] + to_column(offset)

    wait(xr.at[0:7], ssem.at[0])
    wait(kt.at[:, 0:240], ssem.at[1])
    wait(vt.at[:, 0:240], ssem.at[2])
    wait(kr.at[0:7], ssem.at[3])
    wait(vr.at[0:7], ssem.at[4])
    wait(ar.at[0:7], ssem.at[5])
    wait(aa.at[0:31], ssem.at[6])
    wait(pr.at[0:15], ssem.at[7])
    wait(nb.at[0, 0, 0:7], ssem.at[8])
    wait(sq_r.at[0:15], ssem.at[9])
    wait(nb.at[0, 0:15], ssem.at[10])
    wait(nb.at[0], ssem.at[11])
    wait(sc_r.at[0:15], ssem.at[12])
    wait(lv_r.at[0:15], ssem.at[13])
    wait(lb_r.at[0:15], ssem.at[14])


def body(
    queries, key_new, value_new, key_cache, value_cache, parents, tokens, hidden, out_weight, final_gain,
    head_weight, past_scores,
):
    any_space = pl.BlockSpec(memory_space=pl.ANY)
    vmem = pl.BlockSpec(memory_space=pltpu.VMEM)
    smem = pl.BlockSpec(memory_space=pltpu.SMEM)
    V = pltpu.VMEM
    scratch = [
        V((16, 1024), BF16), V((16, 1024), BF16), V((16, 1024), BF16),
        V((16, 16, 1024), BF16), V((16, 16, 1024), BF16),
        V((16, 512), BF16), V((512, 512), BF16), V((501, 8192), BF16), V((256, 501), F32),
        V((8, 256, 128), BF16), V((8, 256, 128), BF16),
        V((16, 640), BF16), V((8, 16, 640), BF16), V((1024, 1024), BF16),
        V((64, 1024), F32), V((64, 128), F32), V((64, 128), F32), V((64, 1024), F32),
        V((8, 16, 512), BF16), V((8, 16, 512), BF16),
        V((2, 16, 256), BF16), V((32, 16, 256), BF16),
        V((16, 16, 512), BF16), V((16, 16, 512), BF16),
        V((8, 4, 16, 1024), BF16), V((8, 4, 16, 1024), BF16),
        V((8, 4, 16, 1024), BF16), V((8, 4, 16, 1024), BF16),
        V((2, 16, 8, 16, 512), BF16),
        V((1, 128), F32), V((16, 1, 128), F32), V((1, 128), F32), V((16, 1, 128), F32),
        V((256, 501), F32), V((256, 1), F32),
        V((8, 128), F32), V((16, 8, 128), F32), V((8, 128), F32), V((16, 8, 128), F32),
        pltpu.SemaphoreType.DMA((9,)), pltpu.SemaphoreType.DMA((14,)), pltpu.SemaphoreType.DMA((15,)),
        pltpu.SemaphoreType.DMA((2, 2)), pltpu.SemaphoreType.DMA((2, 2)),
        pltpu.SemaphoreType.DMA((2, 4, 2)), pltpu.SemaphoreType.DMA((2, 4, 2)),
    ]
    return pl.pallas_call(
        kernel,
        out_shape=(
            jax.ShapeDtypeStruct((16, 16, 1024), BF16),
            jax.ShapeDtypeStruct((16, 16, 1024), BF16),
            jax.ShapeDtypeStruct((256, 501), F32),
        ),
        in_specs=[any_space] * 5 + [smem] * 2 + [any_space] * 2 + [vmem] + [any_space] * 2,
        out_specs=(vmem, vmem, vmem),
        scratch_shapes=scratch,
        compiler_params=pltpu.CompilerParams(
            collective_id=0, has_side_effects=True, vmem_limit_bytes=48 * 1024 * 1024
        ),
        name="beam_step",
    )(
        queries, key_new, value_new, key_cache, value_cache, parents, tokens, hidden, out_weight,
        final_gain.reshape(1, 512), head_weight, past_scores,
    )


def solution(mesh):
    in_specs = (
        P("batch", None), P("batch", None), P("batch", None),
        P("batch", "vocab", None), P("batch", "vocab", None),
        P(), P(), P(None, "batch"), P("vocab", "batch"), P("batch"),
        P(("batch", "vocab"), None), P(None, ("batch", "vocab")),
    )
    out_specs = (P("batch", "vocab", None), P("batch", "vocab", None), P(None, ("batch", "vocab")))
    return jax.shard_map(body, mesh=mesh, in_specs=in_specs, out_specs=out_specs, check_vma=False)
```

```python
import functools

import jax
import jax.numpy as jnp
from jax import lax
from jax.experimental import pallas as pl
from jax.experimental.pallas import tpu as pltpu
from jax.sharding import PartitionSpec as P

D = 8192
HEAD_DIM = 128
MESH = pl.DeviceIdType.MESH
F32 = jnp.float32
BF16 = jnp.bfloat16
NT = (((1,), (1,)), ((), ()))

BULK_EARLY_K = (1, 7, 2, 6, 4)
BULK_MID_V = (4,)
BULK_LATE_K = (3, 5)
BULK_LATE_V = (1, 7, 2, 6, 3, 5)
AWAY = (0, 1, 7, 2, 6, 3, 5, 4)


def iota(shape, axis):
    return lax.broadcasted_iota(jnp.int32, shape, axis)


def kernel(
    q_ref, kn_ref, vn_ref, kc_ref, vc_ref, par_ref, pl_ref, tl_ref, hid_ref, w_ref, gain_ref, hw_ref, past_ref,
    nk_ref, nv_ref, cand_ref,
    q_v, kn_v, vn_v, kc_v, vc_v, par_s, par_v, tok_v, hid_v, w_v, gain_v, hw_v, past_v,
    kt, vt, xs, xr, perm, qp, kn_s, vn_s, w_s, o_new, o_s, rs, ar, a_s, aa, ps, pr,
    ks, vs, kr, vr, nb, sq_s, sq_r, sc_s, sc_r, acc, nk_s, nv_s, lv_s, lv_r, lb_s, lb_r,
    lsem, rsem, ssem, s1, s2, t1, t2,
):
    b = lax.axis_index("batch")
    v = lax.axis_index("vocab")
    z, c = b // 2, b % 2
    kind = (c + z) % 2
    g, h = v // 2, v % 2
    x, y = v // 4, v % 4

    def same_kind(zz):
        return 2 * zz + (kind + zz) % 2

    def send(src, dst, send_sem, recv_sem, dev):
        pltpu.make_async_remote_copy(
            src_ref=src, dst_ref=dst, send_sem=send_sem, recv_sem=recv_sem,
            device_id=dev, device_id_type=MESH,
        ).start()

    def wait(ref, sem):
        pltpu.make_async_copy(ref, ref, sem).wait()

    pending = []

    def drain():
        for ref, sem in pending:
            wait(ref, sem)
        for i in list(left):
            arrived(i)

    def arrived(i):
        local[i].wait()
        left.remove(i)

    local = [
        pltpu.make_async_copy(q_ref.at[:, pl.ds(pl.multiple_of(g * 1024, 1024), 1024)], q_v, lsem.at[0]),
        pltpu.make_async_copy(kn_ref, kn_v, lsem.at[1]),
        pltpu.make_async_copy(vn_ref, vn_v, lsem.at[2]),
        pltpu.make_async_copy(kc_ref, kc_v, lsem.at[3]),
        pltpu.make_async_copy(vc_ref, vc_v, lsem.at[4]),
        pltpu.make_async_copy(past_ref, past_v, lsem.at[5]),
        pltpu.make_async_copy(w_ref, w_v, lsem.at[6]),
        pltpu.make_async_copy(hid_ref.at[pl.ds(pl.multiple_of(v * 16, 16), 16)], hid_v, lsem.at[7]),
        pltpu.make_async_copy(hw_ref, hw_v, lsem.at[8]),
        pltpu.make_async_copy(par_ref, par_s, lsem.at[9]),
        pltpu.make_async_copy(pl_ref, par_v, lsem.at[10]),
        pltpu.make_async_copy(tl_ref, tok_v, lsem.at[11]),
        pltpu.make_async_copy(gain_ref, gain_v, lsem.at[12]),
    ]
    left = list(range(len(local)))
    for copy in local:
        copy.start()

    bar = pltpu.get_barrier_semaphore()

    def greet(d, _):
        pl.semaphore_signal(bar, inc=1, device_id=(b, (v + d) % 16), device_id_type=MESH)
        pl.semaphore_signal(bar, inc=1, device_id=((b + d) % 16, v), device_id_type=MESH)
        return 0

    def greet_pair(d, _):
        pl.semaphore_signal(
            bar, inc=1, device_id=(2 * ((z + d) % 8) + c, 2 * g + 1 - h), device_id_type=MESH
        )
        return 0

    lax.fori_loop(1, 16, greet, 0)
    lax.fori_loop(1, 8, greet_pair, 0)

    for i in range(3):
        arrived(i)
    lane_g = pl.ds(pl.multiple_of(g * 128, 128), 128)
    packed = jnp.concatenate(
        [q_v[...].astype(F32), kn_v[:, lane_g].astype(F32), vn_v[:, lane_g].astype(F32)], axis=1
    )
    upper = h.astype(F32)
    packed = packed[0:8] * (1.0 - upper) + packed[8:16] * upper
    packed = jnp.concatenate([packed[:, :640], packed[:, 640:]], axis=0).astype(BF16)
    xs[...] = packed
    xr[z] = packed

    pl.semaphore_wait(bar, 37)

    def send_query(d, _):
        zz = (z + d) % 8
        send(xs, xr.at[z], ssem.at[0], rsem.at[0], (same_kind(zz), v))
        return 0

    lax.fori_loop(1, 8, send_query, 0)
    pending.append((xr.at[0:7], ssem.at[0]))

    def cache_part(ref, target):
        rows = pl.ds(pl.multiple_of((target % 2) * 8, 8), 8)
        return ref.at[rows, :, pl.ds(pl.multiple_of((target // 2) * 128, 128), 128)]

    my_pos = pl.ds(pl.multiple_of(v * 16, 16), 16)

    def turn(ref, out, i):
        def step(d, _):
            t = (v + d) % 16
            send(cache_part(ref, t), out.at[:, my_pos, :], ssem.at[i], rsem.at[i], (b, t))
            return 0

        lax.fori_loop(1, 16, step, 0)
        pltpu.make_async_copy(cache_part(ref, v), out.at[:, my_pos, :], rsem.at[i]).start()

    turn(kc_ref, kt, 1)
    pending.append((kt.at[:, 0:240], ssem.at[1]))
    turn(vc_ref, vt, 2)
    pending.append((vt.at[:, 0:240], ssem.at[2]))

    for i in (3, 4, 9):
        arrived(i)

    def stage(zz, _):
        base = same_kind(zz) * 16
        count = jnp.int32(0)
        rows = [jnp.int32(0)] * 4
        for r in range(16):
            mine = (par_s[base + r] // 32 == z).astype(jnp.int32)
            for k in range(4):
                rows[k] = jnp.where(count * mine + mine == k + 1, r, rows[k])
            count = count + mine
        for k in range(4):
            ks[zz, k] = kc_v[rows[k]]
            vs[zz, k] = vc_v[rows[k]]
        return 0

    lax.fori_loop(0, 8, stage, 0)
    kr[z] = ks[z]
    vr[z] = vs[z]

    def bulk(src, dst, i, distances):
        for d in distances:
            zz = (z + d) % 8
            send(src.at[zz], dst.at[z], ssem.at[i], rsem.at[i], (same_kind(zz), v))

    bulk(ks, kr, 3, BULK_EARLY_K)

    lanes = iota((128, 1024), 1)
    wanted = (lanes % 128) * 8 + lanes // 128
    subs = iota((128, 1024), 0)

    def build(t, _):
        perm[pl.ds(pl.multiple_of(t * 128, 128), 128), :] = (subs + t * 128 == wanted).astype(F32).astype(BF16)
        return 0

    lax.fori_loop(0, 8, build, 0)
    k64 = iota((64, 64), 0)
    swap = (iota((64, 64), 1) == (k64 % 8) * 8 + k64 // 8).astype(F32).astype(BF16)

    for i in (5, 10, 11):
        arrived(i)
    chosen = (iota((256, 256), 0) == par_v[...]).astype(F32)
    of_parent = jnp.dot(past_v[...], chosen, precision=lax.Precision.HIGHEST, preferred_element_type=F32)
    own_token = iota((501, 256), 0) == tok_v[...] - (b * 16 + v) * 501
    acc[496:504] = jnp.zeros((8, 256), F32)
    acc[0:501] = jnp.where(own_token, of_parent, 0.0)
    picked = jnp.sum(acc[...], axis=0, keepdims=True)
    acc[496:504] = jnp.full((8, 256), -1e30, F32)

    wait(xr.at[0:7], rsem.at[0])
    got = xr[...].astype(F32)
    got = jnp.concatenate(
        [got[:, 0:8, :].reshape(64, 640), got[:, 8:16, :].reshape(64, 640)], axis=1
    ).astype(BF16)
    got = jnp.dot(swap, got, preferred_element_type=F32)
    kn_s[...] = got[:, 1024:1152]
    vn_s[...] = got[:, 1152:1280]
    qp[...] = jnp.dot(got[:, :1024].astype(BF16), perm[...], preferred_element_type=F32)
    wait(kt, rsem.at[1])
    lane256 = iota((64, 256), 1)

    def weigh(r, _):
        rows = pl.ds(pl.multiple_of(r * 8, 8), 8)
        qr = qp[rows, :]
        qf = jnp.concatenate([qr[:, j * 128:(j + 1) * 128] for j in range(8)], axis=0)
        new_key = jnp.concatenate([kn_s[rows, :]] * 8, axis=0)
        new_value = jnp.concatenate([vn_s[rows, :]] * 8, axis=0)
        s = lax.dot_general(qf.astype(BF16), kt[r], NT, preferred_element_type=F32)
        s_new = jnp.sum(qf * new_key, axis=1, keepdims=True)
        s = jnp.where(lane256 == 255, s_new, s) * HEAD_DIM ** (-0.5)
        e = jnp.exp(s - jnp.max(s, axis=1, keepdims=True))
        wf = (e / jnp.sum(e, axis=1, keepdims=True)).astype(BF16).astype(F32)
        w_s[r] = jnp.where(lane256 == 255, 0.0, wf).astype(BF16)
        o_new[r] = wf[:, 255:256] * new_value
        return 0

    lax.fori_loop(0, 8, weigh, 0, unroll=4)
    wait(vt, rsem.at[2])

    def mix(r, _):
        rows = pl.ds(pl.multiple_of(r * 8, 8), 8)
        o = jnp.dot(w_s[r], vt[r], preferred_element_type=F32) + o_new[r]
        o_s[rows, :] = jnp.concatenate([o[j * 8:(j + 1) * 8] for j in range(8)], axis=1)
        return 0

    lax.fori_loop(0, 8, mix, 0, unroll=4)
    o = lax.dot_general(o_s[...].astype(BF16), perm[...], NT, preferred_element_type=F32).astype(BF16)
    o = jnp.dot(swap, o, preferred_element_type=F32).reshape(8, 8, 1024)
    rs[...] = jnp.concatenate([o[:, :, :512], o[:, :, 512:]], axis=1).astype(BF16)
    ar[z] = rs[z]

    def send_back(d, _):
        zz = (z + d) % 8
        send(rs.at[zz], ar.at[z], ssem.at[5], rsem.at[5], (same_kind(zz), v))
        return 0

    lax.fori_loop(1, 8, send_back, 0)
    pending.append((ar.at[0:7], ssem.at[5]))
    sub16 = iota((16, 512), 0)
    beam = jnp.zeros((16, 512), jnp.int32)
    for r in range(8):
        beam = jnp.where(sub16 % 8 == r, par_s[b * 16 + h * 8 + r] // 32, beam)
    wait(ar.at[0:7], rsem.at[5])
    att = jnp.zeros((16, 512), F32)
    for p in range(8):
        att = jnp.where(beam == p, ar[p].astype(F32), att)
    for hh in range(2):
        part = att[hh * 8:hh * 8 + 8]
        a_s[hh] = jnp.concatenate([part[:, :256], part[:, 256:]], axis=0).astype(BF16)
    aa[16 * c + 2 * z + h] = a_s[h]

    slot = aa.at[16 * c + 2 * z + h]
    send(a_s.at[1 - h], slot, ssem.at[6], rsem.at[6], (b, 2 * g + 1 - h))

    def spread(d, _):
        zz = (z + d) % 8
        for hh in range(2):
            send(a_s.at[hh], slot, ssem.at[6], rsem.at[6], (2 * zz + c, 2 * g + hh))
        return 0

    lax.fori_loop(1, 8, spread, 0)
    pending.append((aa.at[0:15], ssem.at[6]))
    for i in (6, 7, 12):
        arrived(i)
    wait(aa.at[0:15], rsem.at[6])
    share = aa.at[pl.ds(16 * c, 16)]
    send(share, share, ssem.at[15], rsem.at[15], (2 * z + 1 - c, v))
    wait(aa.at[0:16], rsem.at[15])
    pending.append((aa.at[0:16], ssem.at[15]))
    rows_in = aa[...].astype(F32)
    rows_in = jnp.concatenate(
        [rows_in[:, 0:8, :].reshape(256, 256), rows_in[:, 8:16, :].reshape(256, 256)], axis=1
    ).astype(BF16)
    ps[...] = jnp.dot(rows_in, w_v[...], preferred_element_type=F32).astype(BF16).reshape(16, 16, 512)
    pr[v] = ps[(v % 2) * 8 + v // 2]

    def send_partial(d, _):
        t = (v + d) % 16
        send(ps.at[(t % 2) * 8 + t // 2], pr.at[v], ssem.at[7], rsem.at[7], (b, t))
        return 0

    lax.fori_loop(1, 16, send_partial, 0)
    pending.append((pr.at[0:15], ssem.at[7]))
    bulk(vs, vr, 4, BULK_MID_V)
    wait(pr.at[0:15], rsem.at[7])
    residual = hid_v[...].astype(F32) + jnp.sum(pr[...].astype(F32), axis=0)
    nb[c, v, 0] = (residual * gain_v[...]).astype(BF16)

    for slot in (1, 2, 3, 4, 5, 6, 7):
        zz = (z - AWAY[slot]) % 8
        send(nb.at[c, v, 0], nb.at[c, v, slot], ssem.at[8], rsem.at[8 if slot < 4 else 14], (2 * zz + c, v))
    pending.append((nb.at[0, 0, 0:7], ssem.at[8]))
    lane256 = iota((16, 256), 1)
    square = jnp.sum(residual * residual, axis=1, keepdims=True)
    square = jnp.where(lane256 == iota((16, 256), 0) + 16 * v, square, 0.0)
    square = jnp.sum(square, axis=0, keepdims=True)
    sq_s[...] = square
    sq_r[b] = square

    def send_square(d, _):
        send(sq_s, sq_r.at[b], ssem.at[9], rsem.at[9], ((b + d) % 16, v))
        return 0

    lax.fori_loop(1, 16, send_square, 0)
    pending.append((sq_r.at[0:15], ssem.at[9]))

    def along(u, axis, d):
        if axis == 0:
            return ((u // 4 + d) % 4) * 4 + u % 4
        return (u // 4) * 4 + (u % 4 + d) % 4

    def piece(u, half, part=None):
        if part is None:
            return nb.at[c, u, 4 * half:4 * half + 4]
        return nb.at[c, u, 4 * half + 2 * part:4 * half + 2 * part + 2]

    def state(ref, axis, d, sem):
        send(ref, ref, ssem.at[10], sem, (b, along(v, axis, d)))

    def sibling(ref):
        send(ref, ref, ssem.at[11], rsem.at[10], (2 * z + 1 - c, v))

    halves = ((1, 0), (0, 1))

    def first(half, order=halves):
        axis = order[half][0]
        state(piece(v, half), axis, 1, s1.at[half, 0])
        state(piece(v, half), axis, -1, s1.at[half, 1])
        state(piece(v, half), axis, 2, s2.at[half])

    def second(half, o):
        u = along(v, halves[half][0], o)
        axis = halves[half][1]
        state(piece(u, half), axis, 1, t1.at[half, o, 0])
        state(piece(u, half), axis, -1, t1.at[half, o, 1])
        if o == 2:
            state(piece(u, half), axis, 2, t2.at[half, o, 0])

    def second_forward(half, o):
        u = along(v, halves[half][0], o)
        axis = halves[half][1]
        wait(piece(u, half), t1.at[half, o, 0])
        state(piece(along(u, axis, -1), half, 0), axis, 1, t2.at[half, o, 0])
        sibling(piece(along(u, axis, -1), half))
        wait(piece(u, half), t1.at[half, o, 1])
        state(piece(along(u, axis, 1), half, 1), axis, -1, t2.at[half, o, 1])
        sibling(piece(along(u, axis, 1), half))

    for half in range(2):
        if half == 0:
            wait(nb.at[0, 0, 0:3], rsem.at[8])
        else:
            wait(nb.at[0, 0, 0:4], rsem.at[14])
        first(half)
        second(half, 0)
        sibling(piece(v, half))
    for half in range(2):
        wait(piece(v, half), s1.at[half, 0])
        second(half, 3)
        wait(piece(v, half), s1.at[half, 1])
        second(half, 1)
        sibling(piece(along(v, halves[half][0], -1), half))
        sibling(piece(along(v, halves[half][0], 1), half))
    bulk(ks, kr, 3, BULK_LATE_K)
    bulk(vs, vr, 4, BULK_LATE_V)
    for half in range(2):
        second_forward(half, 0)
    for half in range(2):
        wait(piece(v, half), s2.at[half])
        second(half, 2)
        sibling(piece(along(v, halves[half][0], 2), half))

    wait(sq_r.at[0:15], rsem.at[9])
    scale = lax.rsqrt(jnp.sum(sq_r[...], axis=0) / D + 1e-05)
    scale = jnp.where(iota((1, 256), 1) // 16 == v, scale, 0.0)
    sc_s[...] = scale
    sc_r[v] = scale

    def send_scale(d, _):
        send(sc_s, sc_r.at[v], ssem.at[12], rsem.at[11], (b, (v + d) % 16))
        return 0

    lax.fori_loop(1, 16, send_scale, 0)
    pending.append((sc_r.at[0:15], ssem.at[12]))
    for o in (3, 1):
        for half in range(2):
            second_forward(half, o)
    for o in (0, 3, 1, 2):
        for half in range(2):
            u = along(v, halves[half][0], o)
            axis = halves[half][1]
            if o == 2:
                for k in range(2):
                    wait(piece(u, half), t1.at[half, o, k])
                    sibling(piece(along(u, axis, 2 * k - 1), half))
                wait(piece(u, half), t2.at[half, o, 0])
            else:
                wait(piece(u, half, 0), t2.at[half, o, 0])
                wait(piece(u, half, 1), t2.at[half, o, 1])
            sibling(piece(along(u, axis, 2), half))

    pending.append((nb.at[0, 0:15], ssem.at[10]))
    pending.append((nb.at[0], ssem.at[11]))

    arrived(8)

    def product(core, slot):
        away = jnp.where(slot % 2 == 1, (slot + 1) // 2, (8 - slot // 2) % 8)
        cols = pl.ds(pl.multiple_of((2 * ((z + away) % 8) + core) * 512, 512), 512)
        return lax.dot_general(
            hw_v[:, cols], nb[core, :, slot].reshape(256, 512), NT, preferred_element_type=F32
        )

    def four(core, first_slot):
        return sum(product(core, first_slot + k) for k in range(1, 4)) + product(core, first_slot)

    acc[0:501] = four(c, 0)
    acc[0:501] += four(c, 4)
    wait(nb.at[0], rsem.at[10])

    acc[0:501] += four(1 - c, 0)
    acc[0:501] += four(1 - c, 4)
    wait(sc_r.at[0:15], rsem.at[11])
    logits = acc[...] * jnp.sum(sc_r[...], axis=0)
    acc[...] = logits
    largest = jnp.max(logits, axis=0, keepdims=True)
    total = jnp.sum(jnp.exp(logits - largest), axis=0, keepdims=True)

    def merged(stats):
        high = jnp.max(stats[:, 0:1], axis=0)
        total = jnp.sum(stats[:, 1:2] * jnp.exp(stats[:, 0:1] - high), axis=0)
        return jnp.concatenate([high, total, jnp.sum(stats[:, 2:4], axis=0)], axis=0)

    stats = jnp.concatenate([largest, total, picked, jnp.zeros((1, 256), F32)], axis=0)
    lv_s[...] = stats
    lv_r[v] = stats

    def send_vocab(d, _):
        send(lv_s, lv_r.at[v], ssem.at[13], rsem.at[12], (b, (v + d) % 16))
        return 0

    lax.fori_loop(1, 16, send_vocab, 0)
    pending.append((lv_r.at[0:15], ssem.at[13]))
    wait(lv_r.at[0:15], rsem.at[12])
    stats = merged(lv_r[...])
    lb_s[...] = stats
    lb_r[b] = stats

    def send_batch(d, _):
        send(lb_s, lb_r.at[b], ssem.at[14], rsem.at[13], ((b + d) % 16, v))
        return 0

    lax.fori_loop(1, 16, send_batch, 0)
    pending.append((lb_r.at[0:15], ssem.at[14]))

    wait(kr.at[0:7], rsem.at[3])
    wait(vr.at[0:7], rsem.at[4])
    last = iota((16, 1024), 0) == jnp.where(v == 15, 15, 99)
    new_keys = kn_v[...].astype(F32)
    new_values = vn_v[...].astype(F32)
    beams = [par_s[b * 16 + r] // 32 for r in range(16)]
    for r in range(16):
        at = jnp.int32(0)
        for earlier in range(r):
            at = at + (beams[earlier] == beams[r]).astype(jnp.int32)
        at = jnp.minimum(at, 3)
        nk_s[r] = jnp.where(last, new_keys[r:r + 1], kr[beams[r], at].astype(F32)).astype(BF16)
        nv_s[r] = jnp.where(last, new_values[r:r + 1], vr[beams[r], at].astype(F32)).astype(BF16)

    results = [
        pltpu.make_async_copy(nk_s, nk_ref, lsem.at[13]),
        pltpu.make_async_copy(nv_s, nv_ref, lsem.at[14]),
    ]
    for copy in results:
        copy.start()
    wait(lb_r.at[0:15], rsem.at[13])
    stats = merged(lb_r[...])
    cand_ref[...] = acc[0:501] + (stats[2:3] - (stats[0:1] + jnp.log(stats[1:2])))

    for copy in results:
        copy.wait()
    pending.append((kr.at[0:7], ssem.at[3]))
    pending.append((vr.at[0:7], ssem.at[4]))
    drain()


def deliver(nk_in, nv_in, cand_in, nk_out, nv_out, cand_out, nk_v, nv_v, cand_v, sem):
    steps = ((nk_in, nk_v, nk_out), (nv_in, nv_v, nv_out), (cand_in, cand_v, cand_out))
    loads = [pltpu.make_async_copy(src, held, sem.at[0, i]) for i, (src, held, _) in enumerate(steps)]
    stores = [pltpu.make_async_copy(held, dst, sem.at[1, i]) for i, (_, held, dst) in enumerate(steps)]
    for load in loads:
        load.start()
    for load, store in zip(loads, stores):
        load.wait()
        store.start()
    for store in stores:
        store.wait()


def body(
    queries, key_new, value_new, key_cache, value_cache, parents, tokens, hidden, out_weight, final_gain,
    head_weight, past_scores,
):
    hbm = pl.BlockSpec(memory_space=pltpu.HBM)
    vmem = pl.BlockSpec(memory_space=pltpu.VMEM)
    V = pltpu.VMEM
    scratch = [
        V((16, 1024), BF16), V((16, 1024), BF16), V((16, 1024), BF16),
        V((16, 16, 1024), BF16), V((16, 16, 1024), BF16),
        pltpu.SMEM((256,), jnp.int32), V((1, 256), jnp.int32), V((1, 256), jnp.int32),
        V((16, 512), BF16), V((512, 512), BF16), V((1, 512), F32),
        V((501, 8192), BF16), V((501, 256), F32),
        V((8, 256, 128), BF16), V((8, 256, 128), BF16),
        V((16, 640), BF16), V((8, 16, 640), BF16), V((1024, 1024), BF16),
        V((64, 1024), F32), V((64, 128), F32), V((64, 128), F32),
        V((8, 64, 256), BF16), V((8, 64, 128), F32), V((64, 1024), F32),
        V((8, 16, 512), BF16), V((8, 16, 512), BF16),
        V((2, 16, 256), BF16), V((32, 16, 256), BF16),
        V((16, 16, 512), BF16), V((16, 16, 512), BF16),
        V((8, 4, 16, 1024), BF16), V((8, 4, 16, 1024), BF16),
        V((8, 4, 16, 1024), BF16), V((8, 4, 16, 1024), BF16),
        V((2, 16, 8, 16, 512), BF16),
        V((1, 256), F32), V((16, 1, 256), F32), V((1, 256), F32), V((16, 1, 256), F32),
        V((504, 256), F32), V((16, 16, 1024), BF16), V((16, 16, 1024), BF16),
        V((4, 256), F32), V((16, 4, 256), F32), V((4, 256), F32), V((16, 4, 256), F32),
        pltpu.SemaphoreType.DMA((15,)), pltpu.SemaphoreType.DMA((16,)), pltpu.SemaphoreType.DMA((16,)),
        pltpu.SemaphoreType.DMA((2, 2)), pltpu.SemaphoreType.DMA((2,)),
        pltpu.SemaphoreType.DMA((2, 4, 2)), pltpu.SemaphoreType.DMA((2, 4, 2)),
    ]
    next_keys, next_values, scores = pl.pallas_call(
        kernel,
        out_shape=(
            jax.ShapeDtypeStruct((16, 16, 1024), BF16),
            jax.ShapeDtypeStruct((16, 16, 1024), BF16),
            jax.ShapeDtypeStruct((501, 256), F32),
        ),
        in_specs=[hbm] * 13,
        out_specs=(hbm, hbm, vmem),
        scratch_shapes=scratch,
        compiler_params=pltpu.CompilerParams(
            collective_id=0, has_side_effects=True, vmem_limit_bytes=62 * 1024 * 1024
        ),
        name="beam_step",
    )(
        queries, key_new, value_new, key_cache, value_cache, parents, parents.reshape(1, 256), tokens.reshape(1, 256),
        hidden, out_weight, final_gain.reshape(1, 512), head_weight, past_scores.T,
    )
    next_keys, next_values, scores = pl.pallas_call(
        deliver,
        out_shape=(
            jax.ShapeDtypeStruct((16, 16, 1024), BF16),
            jax.ShapeDtypeStruct((16, 16, 1024), BF16),
            jax.ShapeDtypeStruct((501, 256), F32),
        ),
        in_specs=[hbm] * 3,
        out_specs=(hbm,) * 3,
        scratch_shapes=[
            V((16, 16, 1024), BF16), V((16, 16, 1024), BF16), V((501, 256), F32),
            pltpu.SemaphoreType.DMA((2, 3)),
        ],
        compiler_params=pltpu.CompilerParams(vmem_limit_bytes=62 * 1024 * 1024),
        name="deliver",
    )(next_keys, next_values, scores)
    return next_keys, next_values, scores.T


def solution(mesh):
    in_specs = (
        P("batch", None), P("batch", None), P("batch", None),
        P("batch", "vocab", None), P("batch", "vocab", None),
        P(), P(), P(None, "batch"), P("vocab", "batch"), P("batch"),
        P(("batch", "vocab"), None), P(None, ("batch", "vocab")),
    )
    out_specs = (P("batch", "vocab", None), P("batch", "vocab", None), P(None, ("batch", "vocab")))
    return jax.shard_map(body, mesh=mesh, in_specs=in_specs, out_specs=out_specs, check_vma=False)
```

```python
import functools

import jax
import jax.numpy as jnp
from jax import lax
from jax.experimental import pallas as pl
from jax.experimental.pallas import tpu as pltpu
from jax.sharding import PartitionSpec as P

D = 8192
HEAD_DIM = 128
MESH = pl.DeviceIdType.MESH
F32 = jnp.float32
BF16 = jnp.bfloat16
NT = (((1,), (1,)), ((), ()))

BULK_EARLY_K = (2, 6)
BULK_EARLY_V = (2, 6)
BULK_BACK_K = (1, 7)
BULK_SPREAD_V = (1, 7)
BULK_MID_K = (4,)
BULK_LATE_K = (3, 5)
BULK_LATE_V = (4, 3, 5)
AWAY = (0, 1, 7, 2, 6, 3, 5, 4)


def iota(shape, axis):
    return lax.broadcasted_iota(jnp.int32, shape, axis)


def kernel(
    q_ref, kn_ref, vn_ref, kc_ref, vc_ref, par_ref, pl_ref, tl_ref, hid_ref, w_ref, gain_ref, hw_ref, past_ref,
    nk_ref, nv_ref, cand_ref,
    q_v, kn_v, vn_v, kc_v, vc_v, par_s, par_v, tok_v, hid_v, w_v, gain_v, hw_v, past_v,
    kt, vt, xs, xr, perm, qp, kn_s, vn_s, w_s, o_new, o_s, rs, ar, a_s, aa, ps, pr,
    ks, vs, kr, vr, nb, sq_s, sq_r, sc_s, sc_r, acc, nk_s, nv_s, lv_s, lv_r, lb_s, lb_r,
    lsem, rsem, ssem, s1, s2, t1, t2,
):
    b = lax.axis_index("batch")
    v = lax.axis_index("vocab")
    z, c = b // 2, b % 2
    kind = (c + z) % 2
    g, h = v // 2, v % 2
    x, y = v // 4, v % 4

    def same_kind(zz):
        return 2 * zz + (kind + zz) % 2

    def send(src, dst, send_sem, recv_sem, dev):
        pltpu.make_async_remote_copy(
            src_ref=src, dst_ref=dst, send_sem=send_sem, recv_sem=recv_sem,
            device_id=dev, device_id_type=MESH,
        ).start()

    def wait(ref, sem):
        pltpu.make_async_copy(ref, ref, sem).wait()

    pending = []

    def drain():
        for ref, sem in pending:
            wait(ref, sem)
        for i in list(left):
            arrived(i)

    def arrived(i):
        local[i].wait()
        left.remove(i)

    bar = pltpu.get_barrier_semaphore()

    def greet(d, _):
        pl.semaphore_signal(bar, inc=1, device_id=(b, (v + d) % 16), device_id_type=MESH)
        return 0

    def greet_batch(d, _):
        pl.semaphore_signal(bar, inc=1, device_id=((b + d) % 16, v), device_id_type=MESH)
        return 0

    def greet_pair(d, _):
        pl.semaphore_signal(
            bar, inc=1, device_id=(2 * ((z + d) % 8) + c, 2 * g + 1 - h), device_id_type=MESH
        )
        return 0

    lax.fori_loop(1, 16, greet, 0)
    lax.fori_loop(1, 16, greet_batch, 0)
    lax.fori_loop(1, 8, greet_pair, 0)

    local = [
        pltpu.make_async_copy(q_ref.at[:, pl.ds(pl.multiple_of(g * 1024, 1024), 1024)], q_v, lsem.at[0]),
        pltpu.make_async_copy(kn_ref, kn_v, lsem.at[1]),
        pltpu.make_async_copy(vn_ref, vn_v, lsem.at[2]),
        pltpu.make_async_copy(kc_ref, kc_v, lsem.at[3]),
        pltpu.make_async_copy(vc_ref, vc_v, lsem.at[4]),
        pltpu.make_async_copy(past_ref, past_v, lsem.at[5]),
        pltpu.make_async_copy(w_ref, w_v, lsem.at[6]),
        pltpu.make_async_copy(hid_ref.at[pl.ds(pl.multiple_of(v * 16, 16), 16)], hid_v, lsem.at[7]),
        pltpu.make_async_copy(hw_ref, hw_v, lsem.at[8]),
        pltpu.make_async_copy(par_ref, par_s, lsem.at[9]),
        pltpu.make_async_copy(pl_ref, par_v, lsem.at[10]),
        pltpu.make_async_copy(tl_ref, tok_v, lsem.at[11]),
        pltpu.make_async_copy(gain_ref, gain_v, lsem.at[12]),
    ]
    left = list(range(len(local)))
    for copy in local:
        copy.start()

    for i in range(3):
        arrived(i)
    lane_g = pl.ds(pl.multiple_of(g * 128, 128), 128)
    packed = jnp.concatenate(
        [q_v[...].astype(F32), kn_v[:, lane_g].astype(F32), vn_v[:, lane_g].astype(F32)], axis=1
    )
    upper = h.astype(F32)
    packed = packed[0:8] * (1.0 - upper) + packed[8:16] * upper
    packed = jnp.concatenate([packed[:, :640], packed[:, 640:]], axis=0).astype(BF16)
    xs[...] = packed
    xr[z] = packed

    pl.semaphore_wait(bar, 37)

    def send_query(d, _):
        zz = (z + d) % 8
        send(xs, xr.at[z], ssem.at[0], rsem.at[0], (same_kind(zz), v))
        return 0

    lax.fori_loop(1, 8, send_query, 0)
    pending.append((xr.at[0:7], ssem.at[0]))

    def cache_part(ref, target):
        rows = pl.ds(pl.multiple_of((target % 2) * 8, 8), 8)
        return ref.at[rows, :, pl.ds(pl.multiple_of((target // 2) * 128, 128), 128)]

    my_pos = pl.ds(pl.multiple_of(v * 16, 16), 16)

    def turn(ref, out, i):
        def step(d, _):
            t = (v + d) % 16
            send(cache_part(ref, t), out.at[:, my_pos, :], ssem.at[i], rsem.at[i], (b, t))
            return 0

        lax.fori_loop(1, 16, step, 0)
        pltpu.make_async_copy(cache_part(ref, v), out.at[:, my_pos, :], rsem.at[i]).start()

    turn(kc_ref, kt, 1)
    pending.append((kt.at[:, 0:240], ssem.at[1]))
    turn(vc_ref, vt, 2)
    pending.append((vt.at[:, 0:240], ssem.at[2]))

    for i in (3, 4, 9):
        arrived(i)

    def stage(zz, _):
        base = same_kind(zz) * 16
        count = jnp.int32(0)
        rows = [jnp.int32(0)] * 4
        for r in range(16):
            mine = (par_s[base + r] // 32 == z).astype(jnp.int32)
            for k in range(4):
                rows[k] = jnp.where(count * mine + mine == k + 1, r, rows[k])
            count = count + mine
        for k in range(4):
            ks[zz, k] = kc_v[rows[k]]
            vs[zz, k] = vc_v[rows[k]]
        return 0

    lax.fori_loop(0, 8, stage, 0)
    kr[z] = ks[z]
    vr[z] = vs[z]

    def bulk(src, dst, i, distances):
        for d in distances:
            zz = (z + d) % 8
            send(src.at[zz], dst.at[z], ssem.at[i], rsem.at[i], (same_kind(zz), v))

    bulk(ks, kr, 3, BULK_EARLY_K)
    bulk(vs, vr, 4, BULK_EARLY_V)

    lanes = iota((128, 1024), 1)
    wanted = (lanes % 128) * 8 + lanes // 128
    subs = iota((128, 1024), 0)

    def build(t, _):
        perm[pl.ds(pl.multiple_of(t * 128, 128), 128), :] = (subs + t * 128 == wanted).astype(F32).astype(BF16)
        return 0

    lax.fori_loop(0, 8, build, 0)
    k64 = iota((64, 64), 0)
    swap = (iota((64, 64), 1) == (k64 % 8) * 8 + k64 // 8).astype(F32).astype(BF16)

    for i in (5, 10, 11):
        arrived(i)
    chosen = (iota((256, 256), 0) == par_v[...]).astype(F32)
    of_parent = jnp.dot(past_v[...], chosen, precision=lax.Precision.HIGHEST, preferred_element_type=F32)
    own_token = iota((501, 256), 0) == tok_v[...] - (b * 16 + v) * 501
    acc[496:504] = jnp.zeros((8, 256), F32)
    acc[0:501] = jnp.where(own_token, of_parent, 0.0)
    picked = jnp.sum(acc[...], axis=0, keepdims=True)
    acc[496:504] = jnp.full((8, 256), -1e30, F32)

    wait(xr.at[0:7], rsem.at[0])
    got = xr[...].astype(F32)
    got = jnp.concatenate(
        [got[:, 0:8, :].reshape(64, 640), got[:, 8:16, :].reshape(64, 640)], axis=1
    ).astype(BF16)
    got = jnp.dot(swap, got, preferred_element_type=F32)
    kn_s[...] = got[:, 1024:1152]
    vn_s[...] = got[:, 1152:1280]
    qp[...] = jnp.dot(got[:, :1024].astype(BF16), perm[...], preferred_element_type=F32)
    wait(kt, rsem.at[1])
    lane256 = iota((64, 256), 1)

    def weigh(r, _):
        rows = pl.ds(pl.multiple_of(r * 8, 8), 8)
        qr = qp[rows, :]
        qf = jnp.concatenate([qr[:, j * 128:(j + 1) * 128] for j in range(8)], axis=0)
        new_key = jnp.concatenate([kn_s[rows, :]] * 8, axis=0)
        new_value = jnp.concatenate([vn_s[rows, :]] * 8, axis=0)
        s = lax.dot_general(qf.astype(BF16), kt[r], NT, preferred_element_type=F32)
        s_new = jnp.sum(qf * new_key, axis=1, keepdims=True)
        s = jnp.where(lane256 == 255, s_new, s) * HEAD_DIM ** (-0.5)
        e = jnp.exp(s - jnp.max(s, axis=1, keepdims=True))
        wf = (e / jnp.sum(e, axis=1, keepdims=True)).astype(BF16).astype(F32)
        w_s[r] = jnp.where(lane256 == 255, 0.0, wf).astype(BF16)
        o_new[r] = wf[:, 255:256] * new_value
        return 0

    lax.fori_loop(0, 8, weigh, 0, unroll=4)
    wait(vt, rsem.at[2])

    def mix(r, _):
        rows = pl.ds(pl.multiple_of(r * 8, 8), 8)
        o = jnp.dot(w_s[r], vt[r], preferred_element_type=F32) + o_new[r]
        o_s[rows, :] = jnp.concatenate([o[j * 8:(j + 1) * 8] for j in range(8)], axis=1)
        return 0

    lax.fori_loop(0, 8, mix, 0, unroll=4)
    o = lax.dot_general(o_s[...].astype(BF16), perm[...], NT, preferred_element_type=F32).astype(BF16)
    o = jnp.dot(swap, o, preferred_element_type=F32).reshape(8, 8, 1024)
    rs[...] = jnp.concatenate([o[:, :, :512], o[:, :, 512:]], axis=1).astype(BF16)
    ar[z] = rs[z]

    def send_back(d, _):
        zz = (z + d) % 8
        send(rs.at[zz], ar.at[z], ssem.at[5], rsem.at[5], (same_kind(zz), v))
        return 0

    lax.fori_loop(1, 8, send_back, 0)
    bulk(ks, kr, 3, BULK_BACK_K)
    pending.append((ar.at[0:7], ssem.at[5]))
    sub16 = iota((16, 512), 0)
    beam = jnp.zeros((16, 512), jnp.int32)
    for r in range(8):
        beam = jnp.where(sub16 % 8 == r, par_s[b * 16 + h * 8 + r] // 32, beam)
    wait(ar.at[0:7], rsem.at[5])
    att = jnp.zeros((16, 512), F32)
    for p in range(8):
        att = jnp.where(beam == p, ar[p].astype(F32), att)
    for hh in range(2):
        part = att[hh * 8:hh * 8 + 8]
        a_s[hh] = jnp.concatenate([part[:, :256], part[:, 256:]], axis=0).astype(BF16)
    aa[16 * c + 2 * z + h] = a_s[h]

    slot = aa.at[16 * c + 2 * z + h]
    send(a_s.at[1 - h], slot, ssem.at[6], rsem.at[6], (b, 2 * g + 1 - h))

    def spread(d, _):
        zz = (z + d) % 8
        for hh in range(2):
            send(a_s.at[hh], slot, ssem.at[6], rsem.at[6], (2 * zz + c, 2 * g + hh))
        return 0

    lax.fori_loop(1, 8, spread, 0)
    bulk(vs, vr, 4, BULK_SPREAD_V)
    pending.append((aa.at[0:15], ssem.at[6]))
    for i in (6, 7, 12):
        arrived(i)
    wait(aa.at[0:15], rsem.at[6])
    share = aa.at[pl.ds(16 * c, 16)]
    send(share, share, ssem.at[15], rsem.at[15], (2 * z + 1 - c, v))
    wait(aa.at[0:16], rsem.at[15])
    pending.append((aa.at[0:16], ssem.at[15]))
    rows_in = aa[...].astype(F32)
    rows_in = jnp.concatenate(
        [rows_in[:, 0:8, :].reshape(256, 256), rows_in[:, 8:16, :].reshape(256, 256)], axis=1
    ).astype(BF16)
    ps[...] = jnp.dot(rows_in, w_v[...], preferred_element_type=F32).astype(BF16).reshape(16, 16, 512)
    pr[v] = ps[(v % 2) * 8 + v // 2]

    def send_partial(d, _):
        t = (v + d) % 16
        send(ps.at[(t % 2) * 8 + t // 2], pr.at[v], ssem.at[7], rsem.at[7], (b, t))
        return 0

    lax.fori_loop(1, 16, send_partial, 0)
    pending.append((pr.at[0:15], ssem.at[7]))
    bulk(ks, kr, 3, BULK_MID_K)
    wait(pr.at[0:15], rsem.at[7])
    residual = hid_v[...].astype(F32) + jnp.sum(pr[...].astype(F32), axis=0)
    nb[c, v, 0] = (residual * gain_v[...]).astype(BF16)

    for slot in (1, 2, 3, 4, 5, 6, 7):
        zz = (z - AWAY[slot]) % 8
        send(nb.at[c, v, 0], nb.at[c, v, slot], ssem.at[8], rsem.at[8 if slot < 5 else 14], (2 * zz + c, v))
    pending.append((nb.at[0, 0, 0:7], ssem.at[8]))

    def send_own(d, _):
        send(nb.at[c, v, 0], nb.at[c, v, 0], ssem.at[10], rsem.at[16], (b, (v + d) % 16))
        return 0

    lax.fori_loop(1, 16, send_own, 0)
    lane256 = iota((16, 256), 1)
    square = jnp.sum(residual * residual, axis=1, keepdims=True)
    square = jnp.where(lane256 == iota((16, 256), 0) + 16 * v, square, 0.0)
    square = jnp.sum(square, axis=0, keepdims=True)
    sq_s[...] = square
    sq_r[b] = square

    def send_square(d, _):
        send(sq_s, sq_r.at[b], ssem.at[9], rsem.at[9], ((b + d) % 16, v))
        return 0

    lax.fori_loop(1, 16, send_square, 0)
    pending.append((sq_r.at[0:15], ssem.at[9]))

    def along(u, axis, d):
        if axis == 0:
            return ((u // 4 + d) % 4) * 4 + u % 4
        return (u // 4) * 4 + (u % 4 + d) % 4

    def piece(u, half, part=None):
        start, size = ((1, 4), (5, 3))[half]
        if part == 0:
            size = 2
        elif part == 1:
            start, size = start + 2, size - 2
        return nb.at[c, u, start:start + size]

    def state(ref, axis, d, sem):
        send(ref, ref, ssem.at[10], sem, (b, along(v, axis, d)))

    def sibling(ref):
        send(ref, ref, ssem.at[11], rsem.at[10], (2 * z + 1 - c, v))

    halves = ((1, 0), (0, 1))

    def first(half, order=halves):
        axis = order[half][0]
        state(piece(v, half), axis, 1, s1.at[half, 0])
        state(piece(v, half), axis, -1, s1.at[half, 1])
        state(piece(v, half), axis, 2, s2.at[half])

    def second(half, o):
        u = along(v, halves[half][0], o)
        axis = halves[half][1]
        state(piece(u, half), axis, 1, t1.at[half, o, 0])
        state(piece(u, half), axis, -1, t1.at[half, o, 1])
        if o == 2:
            state(piece(u, half), axis, 2, t2.at[half, o, 0])

    def second_forward(half, o):
        u = along(v, halves[half][0], o)
        axis = halves[half][1]
        wait(piece(u, half), t1.at[half, o, 0])
        state(piece(along(u, axis, -1), half, 0), axis, 1, t2.at[half, o, 0])
        sibling(piece(along(u, axis, -1), half))
        wait(piece(u, half), t1.at[half, o, 1])
        state(piece(along(u, axis, 1), half, 1), axis, -1, t2.at[half, o, 1])
        sibling(piece(along(u, axis, 1), half))

    for half in range(2):
        if half == 0:
            wait(nb.at[0, 0, 0:4], rsem.at[8])
        else:
            wait(nb.at[0, 0, 0:3], rsem.at[14])
        first(half)
        second(half, 0)
        sibling(piece(v, half))
    bulk(ks, kr, 3, BULK_LATE_K)
    bulk(vs, vr, 4, BULK_LATE_V)
    wait(nb.at[0, 0:15, 0], rsem.at[16])
    sibling(nb.at[c, :, 0])
    for half in range(2):
        wait(piece(v, half), s1.at[half, 0])
        second(half, 3)
        wait(piece(v, half), s1.at[half, 1])
        second(half, 1)
        sibling(piece(along(v, halves[half][0], -1), half))
        sibling(piece(along(v, halves[half][0], 1), half))
    for half in range(2):
        second_forward(half, 0)
    for half in range(2):
        wait(piece(v, half), s2.at[half])
        second(half, 2)
        sibling(piece(along(v, halves[half][0], 2), half))

    wait(sq_r.at[0:15], rsem.at[9])
    scale = lax.rsqrt(jnp.sum(sq_r[...], axis=0) / D + 1e-05)
    scale = jnp.where(iota((1, 256), 1) // 16 == v, scale, 0.0)
    sc_s[...] = scale
    sc_r[v] = scale

    def send_scale(d, _):
        send(sc_s, sc_r.at[v], ssem.at[12], rsem.at[11], (b, (v + d) % 16))
        return 0

    lax.fori_loop(1, 16, send_scale, 0)
    pending.append((sc_r.at[0:15], ssem.at[12]))
    for o in (3, 1):
        for half in range(2):
            second_forward(half, o)
    for o in (0, 3, 1, 2):
        for half in range(2):
            u = along(v, halves[half][0], o)
            axis = halves[half][1]
            if o == 2:
                for k in range(2):
                    wait(piece(u, half), t1.at[half, o, k])
                    sibling(piece(along(u, axis, 2 * k - 1), half))
                wait(piece(u, half), t2.at[half, o, 0])
            else:
                wait(piece(u, half, 0), t2.at[half, o, 0])
                wait(piece(u, half, 1), t2.at[half, o, 1])
            sibling(piece(along(u, axis, 2), half))

    pending.append((nb.at[0, 0:15], ssem.at[10]))
    pending.append((nb.at[0], ssem.at[11]))

    arrived(8)

    def product(core, slot):
        away = jnp.where(slot % 2 == 1, (slot + 1) // 2, (8 - slot // 2) % 8)
        cols = pl.ds(pl.multiple_of((2 * ((z + away) % 8) + core) * 512, 512), 512)
        return lax.dot_general(
            hw_v[:, cols], nb[core, :, slot].reshape(256, 512), NT, preferred_element_type=F32
        )

    def four(core, first_slot):
        return sum(product(core, first_slot + k) for k in range(1, 4)) + product(core, first_slot)

    acc[0:501] = four(c, 0)
    acc[0:501] += four(c, 4)
    wait(nb.at[0], rsem.at[10])

    acc[0:501] += four(1 - c, 0)
    acc[0:501] += four(1 - c, 4)
    wait(sc_r.at[0:15], rsem.at[11])
    logits = acc[...] * jnp.sum(sc_r[...], axis=0)
    acc[...] = logits
    largest = jnp.max(logits, axis=0, keepdims=True)
    total = jnp.sum(jnp.exp(logits - largest), axis=0, keepdims=True)

    def merged(stats):
        high = jnp.max(stats[:, 0:1], axis=0)
        total = jnp.sum(stats[:, 1:2] * jnp.exp(stats[:, 0:1] - high), axis=0)
        return jnp.concatenate([high, total, jnp.sum(stats[:, 2:4], axis=0)], axis=0)

    stats = jnp.concatenate([largest, total, picked, jnp.zeros((1, 256), F32)], axis=0)
    lv_s[...] = stats
    lv_r[v] = stats

    def send_vocab(d, _):
        send(lv_s, lv_r.at[v], ssem.at[13], rsem.at[12], (b, (v + d) % 16))
        return 0

    lax.fori_loop(1, 16, send_vocab, 0)
    pending.append((lv_r.at[0:15], ssem.at[13]))
    wait(lv_r.at[0:15], rsem.at[12])
    stats = merged(lv_r[...])
    lb_s[...] = stats
    lb_r[b] = stats

    def send_batch(d, _):
        send(lb_s, lb_r.at[b], ssem.at[14], rsem.at[13], ((b + d) % 16, v))
        return 0

    lax.fori_loop(1, 16, send_batch, 0)
    pending.append((lb_r.at[0:15], ssem.at[14]))

    wait(kr.at[0:7], rsem.at[3])
    wait(vr.at[0:7], rsem.at[4])
    last = iota((16, 1024), 0) == jnp.where(v == 15, 15, 99)
    new_keys = kn_v[...].astype(F32)
    new_values = vn_v[...].astype(F32)
    beams = [par_s[b * 16 + r] // 32 for r in range(16)]
    for r in range(16):
        at = jnp.int32(0)
        for earlier in range(r):
            at = at + (beams[earlier] == beams[r]).astype(jnp.int32)
        at = jnp.minimum(at, 3)
        nk_s[r] = jnp.where(last, new_keys[r:r + 1], kr[beams[r], at].astype(F32)).astype(BF16)
        nv_s[r] = jnp.where(last, new_values[r:r + 1], vr[beams[r], at].astype(F32)).astype(BF16)

    results = [
        pltpu.make_async_copy(nk_s, nk_ref, lsem.at[13]),
        pltpu.make_async_copy(nv_s, nv_ref, lsem.at[14]),
    ]
    for copy in results:
        copy.start()
    wait(lb_r.at[0:15], rsem.at[13])
    stats = merged(lb_r[...])
    cand_ref[...] = acc[0:501] + (stats[2:3] - (stats[0:1] + jnp.log(stats[1:2])))

    for copy in results:
        copy.wait()
    pending.append((kr.at[0:7], ssem.at[3]))
    pending.append((vr.at[0:7], ssem.at[4]))
    drain()


def deliver(nk_in, nv_in, cand_in, nk_out, nv_out, cand_out, nk_v, nv_v, cand_v, sem):
    steps = ((nk_in, nk_v, nk_out), (nv_in, nv_v, nv_out), (cand_in, cand_v, cand_out))
    loads = [pltpu.make_async_copy(src, held, sem.at[0, i]) for i, (src, held, _) in enumerate(steps)]
    stores = [pltpu.make_async_copy(held, dst, sem.at[1, i]) for i, (_, held, dst) in enumerate(steps)]
    for load in loads:
        load.start()
    for load, store in zip(loads, stores):
        load.wait()
        store.start()
    for store in stores:
        store.wait()


def body(
    queries, key_new, value_new, key_cache, value_cache, parents, tokens, hidden, out_weight, final_gain,
    head_weight, past_scores,
):
    hbm = pl.BlockSpec(memory_space=pltpu.HBM)
    vmem = pl.BlockSpec(memory_space=pltpu.VMEM)
    V = pltpu.VMEM
    scratch = [
        V((16, 1024), BF16), V((16, 1024), BF16), V((16, 1024), BF16),
        V((16, 16, 1024), BF16), V((16, 16, 1024), BF16),
        pltpu.SMEM((256,), jnp.int32), V((1, 256), jnp.int32), V((1, 256), jnp.int32),
        V((16, 512), BF16), V((512, 512), BF16), V((1, 512), F32),
        V((501, 8192), BF16), V((501, 256), F32),
        V((8, 256, 128), BF16), V((8, 256, 128), BF16),
        V((16, 640), BF16), V((8, 16, 640), BF16), V((1024, 1024), BF16),
        V((64, 1024), F32), V((64, 128), F32), V((64, 128), F32),
        V((8, 64, 256), BF16), V((8, 64, 128), F32), V((64, 1024), F32),
        V((8, 16, 512), BF16), V((8, 16, 512), BF16),
        V((2, 16, 256), BF16), V((32, 16, 256), BF16),
        V((16, 16, 512), BF16), V((16, 16, 512), BF16),
        V((8, 4, 16, 1024), BF16), V((8, 4, 16, 1024), BF16),
        V((8, 4, 16, 1024), BF16), V((8, 4, 16, 1024), BF16),
        V((2, 16, 8, 16, 512), BF16),
        V((1, 256), F32), V((16, 1, 256), F32), V((1, 256), F32), V((16, 1, 256), F32),
        V((504, 256), F32), V((16, 16, 1024), BF16), V((16, 16, 1024), BF16),
        V((4, 256), F32), V((16, 4, 256), F32), V((4, 256), F32), V((16, 4, 256), F32),
        pltpu.SemaphoreType.DMA((15,)), pltpu.SemaphoreType.DMA((17,)), pltpu.SemaphoreType.DMA((16,)),
        pltpu.SemaphoreType.DMA((2, 2)), pltpu.SemaphoreType.DMA((2,)),
        pltpu.SemaphoreType.DMA((2, 4, 2)), pltpu.SemaphoreType.DMA((2, 4, 2)),
    ]
    next_keys, next_values, scores = pl.pallas_call(
        kernel,
        out_shape=(
            jax.ShapeDtypeStruct((16, 16, 1024), BF16),
            jax.ShapeDtypeStruct((16, 16, 1024), BF16),
            jax.ShapeDtypeStruct((501, 256), F32),
        ),
        in_specs=[hbm] * 13,
        out_specs=(hbm, hbm, vmem),
        scratch_shapes=scratch,
        compiler_params=pltpu.CompilerParams(
            collective_id=0, has_side_effects=True, vmem_limit_bytes=62 * 1024 * 1024
        ),
        name="beam_step",
    )(
        queries, key_new, value_new, key_cache, value_cache, parents, parents.reshape(1, 256), tokens.reshape(1, 256),
        hidden, out_weight, final_gain.reshape(1, 512), head_weight, past_scores.T,
    )
    next_keys, next_values, scores = pl.pallas_call(
        deliver,
        out_shape=(
            jax.ShapeDtypeStruct((16, 16, 1024), BF16),
            jax.ShapeDtypeStruct((16, 16, 1024), BF16),
            jax.ShapeDtypeStruct((501, 256), F32),
        ),
        in_specs=[hbm] * 3,
        out_specs=(hbm,) * 3,
        scratch_shapes=[
            V((16, 16, 1024), BF16), V((16, 16, 1024), BF16), V((501, 256), F32),
            pltpu.SemaphoreType.DMA((2, 3)),
        ],
        compiler_params=pltpu.CompilerParams(vmem_limit_bytes=62 * 1024 * 1024),
        name="deliver",
    )(next_keys, next_values, scores)
    return next_keys, next_values, scores.T


def solution(mesh):
    in_specs = (
        P("batch", None), P("batch", None), P("batch", None),
        P("batch", "vocab", None), P("batch", "vocab", None),
        P(), P(), P(None, "batch"), P("vocab", "batch"), P("batch"),
        P(("batch", "vocab"), None), P(None, ("batch", "vocab")),
    )
    out_specs = (P("batch", "vocab", None), P("batch", "vocab", None), P(None, ("batch", "vocab")))
    return jax.shard_map(body, mesh=mesh, in_specs=in_specs, out_specs=out_specs, check_vma=False)
```

```python
import functools

import jax
import jax.numpy as jnp
from jax import lax
from jax.experimental import pallas as pl
from jax.experimental.pallas import tpu as pltpu
from jax.sharding import PartitionSpec as P

D = 8192
HEAD_DIM = 128
MESH = pl.DeviceIdType.MESH
F32 = jnp.float32
BF16 = jnp.bfloat16
NT = (((1,), (1,)), ((), ()))

BULK_EARLY_K = (2, 6)
BULK_EARLY_V = (2, 6)
BULK_BACK_K = (1, 7)
BULK_SPREAD_V = (1, 7)
BULK_MID_K = (4,)
BULK_LATE_K = (3, 5)
BULK_LATE_V = (4, 3, 5)
AWAY = (0, 1, 7, 2, 6, 3, 5, 4)


def iota(shape, axis):
    return lax.broadcasted_iota(jnp.int32, shape, axis)


def kernel(
    q_ref, kn_ref, vn_ref, kc_ref, vc_ref, par_ref, pl_ref, tl_ref, hid_ref, w_ref, gain_ref, hw_ref, past_ref,
    nk_ref, nv_ref, logit_ref, offset_ref,
    q_v, kn_v, vn_v, kc_v, vc_v, par_s, par_v, tok_v, hid_v, w_v, gain_v, hw_v, past_v,
    kt, vt, xs, xr, perm, qp, kn_s, vn_s, w_s, o_new, o_s, rs, ar, a_s, aa, ps, pr,
    ks, vs, kr, vr, nb, sq_s, sq_r, sc_s, sc_r, acc, nk_s, nv_s, lv_s, lv_r, lb_s, lb_r,
    lsem, rsem, ssem, s1, s2, t1, t2,
):
    b = lax.axis_index("batch")
    v = lax.axis_index("vocab")
    z, c = b // 2, b % 2
    kind = (c + z) % 2
    g, h = v // 2, v % 2
    x, y = v // 4, v % 4

    def same_kind(zz):
        return 2 * zz + (kind + zz) % 2

    def send(src, dst, send_sem, recv_sem, dev):
        pltpu.make_async_remote_copy(
            src_ref=src, dst_ref=dst, send_sem=send_sem, recv_sem=recv_sem,
            device_id=dev, device_id_type=MESH,
        ).start()

    def wait(ref, sem):
        pltpu.make_async_copy(ref, ref, sem).wait()

    pending = []

    def drain():
        for ref, sem in pending:
            wait(ref, sem)
        for i in list(left):
            arrived(i)

    def arrived(i):
        local[i].wait()
        left.remove(i)

    bar = pltpu.get_barrier_semaphore()

    def greet(d, _):
        pl.semaphore_signal(bar, inc=1, device_id=(b, (v + d) % 16), device_id_type=MESH)
        return 0

    def greet_batch(d, _):
        pl.semaphore_signal(bar, inc=1, device_id=((b + d) % 16, v), device_id_type=MESH)
        return 0

    def greet_pair(d, _):
        pl.semaphore_signal(
            bar, inc=1, device_id=(2 * ((z + d) % 8) + c, 2 * g + 1 - h), device_id_type=MESH
        )
        return 0

    lax.fori_loop(1, 16, greet, 0)
    lax.fori_loop(1, 16, greet_batch, 0)
    lax.fori_loop(1, 8, greet_pair, 0)

    local = [
        pltpu.make_async_copy(q_ref.at[:, pl.ds(pl.multiple_of(g * 1024, 1024), 1024)], q_v, lsem.at[0]),
        pltpu.make_async_copy(kn_ref, kn_v, lsem.at[1]),
        pltpu.make_async_copy(vn_ref, vn_v, lsem.at[2]),
        pltpu.make_async_copy(kc_ref, kc_v, lsem.at[3]),
        pltpu.make_async_copy(vc_ref, vc_v, lsem.at[4]),
        pltpu.make_async_copy(past_ref, past_v, lsem.at[5]),
        pltpu.make_async_copy(w_ref, w_v, lsem.at[6]),
        pltpu.make_async_copy(hid_ref.at[pl.ds(pl.multiple_of(v * 16, 16), 16)], hid_v, lsem.at[7]),
        pltpu.make_async_copy(hw_ref, hw_v, lsem.at[8]),
        pltpu.make_async_copy(par_ref, par_s, lsem.at[9]),
        pltpu.make_async_copy(pl_ref, par_v, lsem.at[10]),
        pltpu.make_async_copy(tl_ref, tok_v, lsem.at[11]),
        pltpu.make_async_copy(gain_ref, gain_v, lsem.at[12]),
    ]
    left = list(range(len(local)))
    for copy in local:
        copy.start()

    for i in range(3):
        arrived(i)
    lane_g = pl.ds(pl.multiple_of(g * 128, 128), 128)
    packed = jnp.concatenate(
        [q_v[...].astype(F32), kn_v[:, lane_g].astype(F32), vn_v[:, lane_g].astype(F32)], axis=1
    )
    upper = h.astype(F32)
    packed = packed[0:8] * (1.0 - upper) + packed[8:16] * upper
    packed = jnp.concatenate([packed[:, :640], packed[:, 640:]], axis=0).astype(BF16)
    xs[...] = packed
    xr[z] = packed

    pl.semaphore_wait(bar, 37)

    def send_query(d, _):
        zz = (z + d) % 8
        send(xs, xr.at[z], ssem.at[0], rsem.at[0], (same_kind(zz), v))
        return 0

    lax.fori_loop(1, 8, send_query, 0)
    pending.append((xr.at[0:7], ssem.at[0]))

    def cache_part(ref, target):
        rows = pl.ds(pl.multiple_of((target % 2) * 8, 8), 8)
        return ref.at[rows, :, pl.ds(pl.multiple_of((target // 2) * 128, 128), 128)]

    my_pos = pl.ds(pl.multiple_of(v * 16, 16), 16)

    def turn(ref, out, i):
        def step(d, _):
            t = (v + d) % 16
            send(cache_part(ref, t), out.at[:, my_pos, :], ssem.at[i], rsem.at[i], (b, t))
            return 0

        lax.fori_loop(1, 16, step, 0)
        pltpu.make_async_copy(cache_part(ref, v), out.at[:, my_pos, :], rsem.at[i]).start()

    turn(kc_ref, kt, 1)
    pending.append((kt.at[:, 0:240], ssem.at[1]))
    turn(vc_ref, vt, 2)
    pending.append((vt.at[:, 0:240], ssem.at[2]))

    for i in (3, 4, 9):
        arrived(i)

    def stage(zz, _):
        base = same_kind(zz) * 16
        count = jnp.int32(0)
        rows = [jnp.int32(0)] * 4
        for r in range(16):
            mine = (par_s[base + r] // 32 == z).astype(jnp.int32)
            for k in range(4):
                rows[k] = jnp.where(count * mine + mine == k + 1, r, rows[k])
            count = count + mine
        for k in range(4):
            ks[zz, k] = kc_v[rows[k]]
            vs[zz, k] = vc_v[rows[k]]
        return 0

    lax.fori_loop(0, 8, stage, 0)
    kr[z] = ks[z]
    vr[z] = vs[z]

    def bulk(src, dst, i, distances):
        for d in distances:
            zz = (z + d) % 8
            send(src.at[zz], dst.at[z], ssem.at[i], rsem.at[i], (same_kind(zz), v))

    bulk(ks, kr, 3, BULK_EARLY_K)
    bulk(vs, vr, 4, BULK_EARLY_V)

    lanes = iota((128, 1024), 1)
    wanted = (lanes % 128) * 8 + lanes // 128
    subs = iota((128, 1024), 0)

    def build(t, _):
        perm[pl.ds(pl.multiple_of(t * 128, 128), 128), :] = (subs + t * 128 == wanted).astype(F32).astype(BF16)
        return 0

    lax.fori_loop(0, 8, build, 0)
    k64 = iota((64, 64), 0)
    swap = (iota((64, 64), 1) == (k64 % 8) * 8 + k64 // 8).astype(F32).astype(BF16)

    for i in (5, 10, 11):
        arrived(i)
    chosen = (iota((256, 256), 0) == par_v[...]).astype(F32)
    of_parent = jnp.dot(past_v[...], chosen, precision=lax.Precision.HIGHEST, preferred_element_type=F32)
    own_token = iota((501, 256), 0) == tok_v[...] - (b * 16 + v) * 501
    acc[496:504] = jnp.zeros((8, 256), F32)
    acc[0:501] = jnp.where(own_token, of_parent, 0.0)
    picked = jnp.sum(acc[...], axis=0, keepdims=True)
    acc[496:504] = jnp.full((8, 256), -1e30, F32)

    wait(xr.at[0:7], rsem.at[0])
    got = xr[...].astype(F32)
    got = jnp.concatenate(
        [got[:, 0:8, :].reshape(64, 640), got[:, 8:16, :].reshape(64, 640)], axis=1
    ).astype(BF16)
    got = jnp.dot(swap, got, preferred_element_type=F32)
    kn_s[...] = got[:, 1024:1152]
    vn_s[...] = got[:, 1152:1280]
    qp[...] = jnp.dot(got[:, :1024].astype(BF16), perm[...], preferred_element_type=F32)
    wait(kt, rsem.at[1])
    lane256 = iota((64, 256), 1)

    def weigh(r, _):
        rows = pl.ds(pl.multiple_of(r * 8, 8), 8)
        qr = qp[rows, :]
        qf = jnp.concatenate([qr[:, j * 128:(j + 1) * 128] for j in range(8)], axis=0)
        new_key = jnp.concatenate([kn_s[rows, :]] * 8, axis=0)
        new_value = jnp.concatenate([vn_s[rows, :]] * 8, axis=0)
        s = lax.dot_general(qf.astype(BF16), kt[r], NT, preferred_element_type=F32)
        s_new = jnp.sum(qf * new_key, axis=1, keepdims=True)
        s = jnp.where(lane256 == 255, s_new, s) * HEAD_DIM ** (-0.5)
        e = jnp.exp(s - jnp.max(s, axis=1, keepdims=True))
        wf = (e / jnp.sum(e, axis=1, keepdims=True)).astype(BF16).astype(F32)
        w_s[r] = jnp.where(lane256 == 255, 0.0, wf).astype(BF16)
        o_new[r] = wf[:, 255:256] * new_value
        return 0

    lax.fori_loop(0, 8, weigh, 0, unroll=4)
    wait(vt, rsem.at[2])

    def mix(r, _):
        rows = pl.ds(pl.multiple_of(r * 8, 8), 8)
        o = jnp.dot(w_s[r], vt[r], preferred_element_type=F32) + o_new[r]
        o_s[rows, :] = jnp.concatenate([o[j * 8:(j + 1) * 8] for j in range(8)], axis=1)
        return 0

    lax.fori_loop(0, 8, mix, 0, unroll=4)
    o = lax.dot_general(o_s[...].astype(BF16), perm[...], NT, preferred_element_type=F32).astype(BF16)
    o = jnp.dot(swap, o, preferred_element_type=F32).reshape(8, 8, 1024)
    rs[...] = jnp.concatenate([o[:, :, :512], o[:, :, 512:]], axis=1).astype(BF16)
    ar[z] = rs[z]

    def send_back(d, _):
        zz = (z + d) % 8
        send(rs.at[zz], ar.at[z], ssem.at[5], rsem.at[5], (same_kind(zz), v))
        return 0

    lax.fori_loop(1, 8, send_back, 0)
    bulk(ks, kr, 3, BULK_BACK_K)
    pending.append((ar.at[0:7], ssem.at[5]))
    sub16 = iota((16, 512), 0)
    beam = jnp.zeros((16, 512), jnp.int32)
    for r in range(8):
        beam = jnp.where(sub16 % 8 == r, par_s[b * 16 + h * 8 + r] // 32, beam)
    wait(ar.at[0:7], rsem.at[5])
    att = jnp.zeros((16, 512), F32)
    for p in range(8):
        att = jnp.where(beam == p, ar[p].astype(F32), att)
    for hh in range(2):
        part = att[hh * 8:hh * 8 + 8]
        a_s[hh] = jnp.concatenate([part[:, :256], part[:, 256:]], axis=0).astype(BF16)
    aa[16 * c + 2 * z + h] = a_s[h]

    slot = aa.at[16 * c + 2 * z + h]
    send(a_s.at[1 - h], slot, ssem.at[6], rsem.at[6], (b, 2 * g + 1 - h))

    def spread(d, _):
        zz = (z + d) % 8
        for hh in range(2):
            send(a_s.at[hh], slot, ssem.at[6], rsem.at[6], (2 * zz + c, 2 * g + hh))
        return 0

    lax.fori_loop(1, 8, spread, 0)
    bulk(vs, vr, 4, BULK_SPREAD_V)
    pending.append((aa.at[0:15], ssem.at[6]))
    for i in (6, 7, 12):
        arrived(i)
    wait(aa.at[0:15], rsem.at[6])
    share = aa.at[pl.ds(16 * c, 16)]
    send(share, share, ssem.at[15], rsem.at[15], (2 * z + 1 - c, v))
    wait(aa.at[0:16], rsem.at[15])
    pending.append((aa.at[0:16], ssem.at[15]))
    rows_in = aa[...].astype(F32)
    rows_in = jnp.concatenate(
        [rows_in[:, 0:8, :].reshape(256, 256), rows_in[:, 8:16, :].reshape(256, 256)], axis=1
    ).astype(BF16)
    ps[...] = jnp.dot(rows_in, w_v[...], preferred_element_type=F32).astype(BF16).reshape(16, 16, 512)
    pr[v] = ps[(v % 2) * 8 + v // 2]

    def send_partial(d, _):
        t = (v + d) % 16
        send(ps.at[(t % 2) * 8 + t // 2], pr.at[v], ssem.at[7], rsem.at[7], (b, t))
        return 0

    lax.fori_loop(1, 16, send_partial, 0)
    pending.append((pr.at[0:15], ssem.at[7]))
    bulk(ks, kr, 3, BULK_MID_K)
    wait(pr.at[0:15], rsem.at[7])
    residual = hid_v[...].astype(F32) + jnp.sum(pr[...].astype(F32), axis=0)
    nb[c, v, 0] = (residual * gain_v[...]).astype(BF16)

    for slot in (1, 2, 3, 4, 5, 6, 7):
        zz = (z - AWAY[slot]) % 8
        send(nb.at[c, v, 0], nb.at[c, v, slot], ssem.at[8], rsem.at[8 if slot < 5 else 14], (2 * zz + c, v))
    pending.append((nb.at[0, 0, 0:7], ssem.at[8]))

    def send_own(d, _):
        send(nb.at[c, v, 0], nb.at[c, v, 0], ssem.at[10], rsem.at[16], (b, (v + d) % 16))
        return 0

    lax.fori_loop(1, 16, send_own, 0)
    lane256 = iota((16, 256), 1)
    square = jnp.sum(residual * residual, axis=1, keepdims=True)
    square = jnp.where(lane256 == iota((16, 256), 0) + 16 * v, square, 0.0)
    square = jnp.sum(square, axis=0, keepdims=True)
    sq_s[...] = square
    sq_r[b] = square

    def send_square(d, _):
        send(sq_s, sq_r.at[b], ssem.at[9], rsem.at[9], ((b + d) % 16, v))
        return 0

    lax.fori_loop(1, 16, send_square, 0)
    pending.append((sq_r.at[0:15], ssem.at[9]))

    def along(u, axis, d):
        if axis == 0:
            return ((u // 4 + d) % 4) * 4 + u % 4
        return (u // 4) * 4 + (u % 4 + d) % 4

    def piece(u, half, part=None):
        start, size = ((1, 4), (5, 3))[half]
        if part == 0:
            size = 2
        elif part == 1:
            start, size = start + 2, size - 2
        return nb.at[c, u, start:start + size]

    def state(ref, axis, d, sem):
        send(ref, ref, ssem.at[10], sem, (b, along(v, axis, d)))

    def sibling(ref, i=10):
        send(ref, ref, ssem.at[11], rsem.at[i], (2 * z + 1 - c, v))

    halves = ((1, 0), (0, 1))

    def first(half, order=halves):
        axis = order[half][0]
        state(piece(v, half), axis, 1, s1.at[half, 0])
        state(piece(v, half), axis, -1, s1.at[half, 1])
        state(piece(v, half), axis, 2, s2.at[half])

    def second(half, o):
        u = along(v, halves[half][0], o)
        axis = halves[half][1]
        state(piece(u, half), axis, 1, t1.at[half, o, 0])
        state(piece(u, half), axis, -1, t1.at[half, o, 1])
        if o == 2:
            state(piece(u, half), axis, 2, t2.at[half, o, 0])

    def second_forward(half, o):
        u = along(v, halves[half][0], o)
        axis = halves[half][1]
        wait(piece(u, half), t1.at[half, o, 0])
        state(piece(along(u, axis, -1), half, 0), axis, 1, t2.at[half, o, 0])
        sibling(piece(along(u, axis, -1), half))
        wait(piece(u, half), t1.at[half, o, 1])
        state(piece(along(u, axis, 1), half, 1), axis, -1, t2.at[half, o, 1])
        sibling(piece(along(u, axis, 1), half))

    for half in range(2):
        if half == 0:
            wait(nb.at[0, 0, 0:4], rsem.at[8])
        else:
            wait(nb.at[0, 0, 0:3], rsem.at[14])
        first(half)
        second(half, 0)
        sibling(piece(v, half))
    bulk(vs, vr, 4, BULK_LATE_V)
    bulk(ks, kr, 3, BULK_LATE_K)
    wait(nb.at[0, 0:15, 0], rsem.at[16])
    sibling(nb.at[c, :, 0], 17)
    for half in range(2):
        wait(piece(v, half), s1.at[half, 0])
        second(half, 3)
        wait(piece(v, half), s1.at[half, 1])
        second(half, 1)
        sibling(piece(along(v, halves[half][0], -1), half))
        sibling(piece(along(v, halves[half][0], 1), half))
    for half in range(2):
        second_forward(half, 0)
    for half in range(2):
        wait(piece(v, half), s2.at[half])
        second(half, 2)
        sibling(piece(along(v, halves[half][0], 2), half))

    wait(sq_r.at[0:15], rsem.at[9])
    scale = lax.rsqrt(jnp.sum(sq_r[...], axis=0) / D + 1e-05)
    scale = jnp.where(iota((1, 256), 1) // 16 == v, scale, 0.0)
    sc_s[...] = scale
    sc_r[v] = scale

    def send_scale(d, _):
        send(sc_s, sc_r.at[v], ssem.at[12], rsem.at[11], (b, (v + d) % 16))
        return 0

    lax.fori_loop(1, 16, send_scale, 0)
    pending.append((sc_r.at[0:15], ssem.at[12]))
    for o in (3, 1):
        for half in range(2):
            second_forward(half, o)
    arrived(8)

    def product(core, slot):
        away = jnp.where(slot % 2 == 1, (slot + 1) // 2, (8 - slot // 2) % 8)
        cols = pl.ds(pl.multiple_of((2 * ((z + away) % 8) + core) * 512, 512), 512)
        return lax.dot_general(
            hw_v[:, cols], nb[core, :, slot].reshape(256, 512), NT, preferred_element_type=F32
        )

    acc[0:501] = product(c, 0)
    wait(nb.at[0, :, 0], rsem.at[17])
    acc[0:501] += product(1 - c, 0)
    for o in (0, 3, 1, 2):
        for half in range(2):
            u = along(v, halves[half][0], o)
            axis = halves[half][1]
            if o == 2:
                for k in range(2):
                    wait(piece(u, half), t1.at[half, o, k])
                    sibling(piece(along(u, axis, 2 * k - 1), half))
                wait(piece(u, half), t2.at[half, o, 0])
            else:
                wait(piece(u, half, 0), t2.at[half, o, 0])
                wait(piece(u, half, 1), t2.at[half, o, 1])
            sibling(piece(along(u, axis, 2), half))

    pending.append((nb.at[0, 0:15], ssem.at[10]))
    pending.append((nb.at[0], ssem.at[11]))

    def several(core, first_slot, count):
        return sum(product(core, first_slot + k) for k in range(1, count)) + product(core, first_slot)

    acc[0:501] += several(c, 1, 4)
    acc[0:501] += several(c, 5, 3)
    wait(nb.at[0, 0:14], rsem.at[10])

    acc[0:501] += several(1 - c, 1, 4)
    acc[0:501] += several(1 - c, 5, 3)
    wait(sc_r.at[0:15], rsem.at[11])
    logits = acc[...] * jnp.sum(sc_r[...], axis=0)
    acc[...] = logits
    results = [
        pltpu.make_async_copy(acc, logit_ref, lsem.at[15]),
        pltpu.make_async_copy(nk_s, nk_ref, lsem.at[13]),
        pltpu.make_async_copy(nv_s, nv_ref, lsem.at[14]),
    ]
    results[0].start()
    largest = jnp.max(logits, axis=0, keepdims=True)
    total = jnp.sum(jnp.exp(logits - largest), axis=0, keepdims=True)

    def merged(stats):
        high = jnp.max(stats[:, 0:1], axis=0)
        total = jnp.sum(stats[:, 1:2] * jnp.exp(stats[:, 0:1] - high), axis=0)
        return jnp.concatenate([high, total, jnp.sum(stats[:, 2:4], axis=0)], axis=0)

    stats = jnp.concatenate([largest, total, picked, jnp.zeros((1, 256), F32)], axis=0)
    lv_s[...] = stats
    lv_r[v] = stats

    def send_vocab(d, _):
        send(lv_s, lv_r.at[v], ssem.at[13], rsem.at[12], (b, (v + d) % 16))
        return 0

    lax.fori_loop(1, 16, send_vocab, 0)
    pending.append((lv_r.at[0:15], ssem.at[13]))
    wait(lv_r.at[0:15], rsem.at[12])
    stats = merged(lv_r[...])
    lb_s[...] = stats
    lb_r[b] = stats

    def send_batch(d, _):
        send(lb_s, lb_r.at[b], ssem.at[14], rsem.at[13], ((b + d) % 16, v))
        return 0

    lax.fori_loop(1, 16, send_batch, 0)
    pending.append((lb_r.at[0:15], ssem.at[14]))

    wait(kr.at[0:7], rsem.at[3])
    wait(vr.at[0:7], rsem.at[4])
    last = iota((16, 1024), 0) == jnp.where(v == 15, 15, 99)
    new_keys = kn_v[...].astype(F32)
    new_values = vn_v[...].astype(F32)
    beams = [par_s[b * 16 + r] // 32 for r in range(16)]
    for r in range(16):
        at = jnp.int32(0)
        for earlier in range(r):
            at = at + (beams[earlier] == beams[r]).astype(jnp.int32)
        at = jnp.minimum(at, 3)
        nk_s[r] = jnp.where(last, new_keys[r:r + 1], kr[beams[r], at].astype(F32)).astype(BF16)
        nv_s[r] = jnp.where(last, new_values[r:r + 1], vr[beams[r], at].astype(F32)).astype(BF16)

    for copy in results[1:]:
        copy.start()
    wait(lb_r.at[0:15], rsem.at[13])
    stats = merged(lb_r[...])
    offset_ref[...] = stats[2:3] - (stats[0:1] + jnp.log(stats[1:2]))

    for copy in results:
        copy.wait()
    pending.append((kr.at[0:7], ssem.at[3]))
    pending.append((vr.at[0:7], ssem.at[4]))
    drain()


def deliver(nk_in, nv_in, logit_in, offset_in, nk_out, nv_out, cand_out, nk_v, nv_v, logit_v, offset_v, cand_v, sem):
    loads = [
        pltpu.make_async_copy(src, held, sem.at[0, i])
        for i, (src, held) in enumerate(((logit_in, logit_v), (nk_in, nk_v), (nv_in, nv_v), (offset_in, offset_v)))
    ]
    stores = [
        pltpu.make_async_copy(held, dst, sem.at[1, i])
        for i, (held, dst) in enumerate(((cand_v, cand_out), (nk_v, nk_out), (nv_v, nv_out)))
    ]
    for load in loads:
        load.start()
    for i in (1, 2, 0):
        loads[i].wait()
        if i == 0:
            loads[3].wait()
            cand_v[...] = logit_v[0:501] + offset_v[...]
        stores[i].start()
    for store in stores:
        store.wait()


def body(
    queries, key_new, value_new, key_cache, value_cache, parents, tokens, hidden, out_weight, final_gain,
    head_weight, past_scores,
):
    hbm = pl.BlockSpec(memory_space=pltpu.HBM)
    vmem = pl.BlockSpec(memory_space=pltpu.VMEM)
    V = pltpu.VMEM
    scratch = [
        V((16, 1024), BF16), V((16, 1024), BF16), V((16, 1024), BF16),
        V((16, 16, 1024), BF16), V((16, 16, 1024), BF16),
        pltpu.SMEM((256,), jnp.int32), V((1, 256), jnp.int32), V((1, 256), jnp.int32),
        V((16, 512), BF16), V((512, 512), BF16), V((1, 512), F32),
        V((501, 8192), BF16), V((501, 256), F32),
        V((8, 256, 128), BF16), V((8, 256, 128), BF16),
        V((16, 640), BF16), V((8, 16, 640), BF16), V((1024, 1024), BF16),
        V((64, 1024), F32), V((64, 128), F32), V((64, 128), F32),
        V((8, 64, 256), BF16), V((8, 64, 128), F32), V((64, 1024), F32),
        V((8, 16, 512), BF16), V((8, 16, 512), BF16),
        V((2, 16, 256), BF16), V((32, 16, 256), BF16),
        V((16, 16, 512), BF16), V((16, 16, 512), BF16),
        V((8, 4, 16, 1024), BF16), V((8, 4, 16, 1024), BF16),
        V((8, 4, 16, 1024), BF16), V((8, 4, 16, 1024), BF16),
        V((2, 16, 8, 16, 512), BF16),
        V((1, 256), F32), V((16, 1, 256), F32), V((1, 256), F32), V((16, 1, 256), F32),
        V((504, 256), F32), V((16, 16, 1024), BF16), V((16, 16, 1024), BF16),
        V((4, 256), F32), V((16, 4, 256), F32), V((4, 256), F32), V((16, 4, 256), F32),
        pltpu.SemaphoreType.DMA((16,)), pltpu.SemaphoreType.DMA((18,)), pltpu.SemaphoreType.DMA((16,)),
        pltpu.SemaphoreType.DMA((2, 2)), pltpu.SemaphoreType.DMA((2,)),
        pltpu.SemaphoreType.DMA((2, 4, 2)), pltpu.SemaphoreType.DMA((2, 4, 2)),
    ]
    next_keys, next_values, logits, offset = pl.pallas_call(
        kernel,
        out_shape=(
            jax.ShapeDtypeStruct((16, 16, 1024), BF16),
            jax.ShapeDtypeStruct((16, 16, 1024), BF16),
            jax.ShapeDtypeStruct((504, 256), F32),
            jax.ShapeDtypeStruct((1, 256), F32),
        ),
        in_specs=[hbm] * 13,
        out_specs=(hbm, hbm, hbm, vmem),
        scratch_shapes=scratch,
        compiler_params=pltpu.CompilerParams(
            collective_id=0, has_side_effects=True, vmem_limit_bytes=62 * 1024 * 1024
        ),
        name="beam_step",
    )(
        queries, key_new, value_new, key_cache, value_cache, parents, parents.reshape(1, 256), tokens.reshape(1, 256),
        hidden, out_weight, final_gain.reshape(1, 512), head_weight, past_scores.T,
    )
    next_keys, next_values, scores = pl.pallas_call(
        deliver,
        out_shape=(
            jax.ShapeDtypeStruct((16, 16, 1024), BF16),
            jax.ShapeDtypeStruct((16, 16, 1024), BF16),
            jax.ShapeDtypeStruct((501, 256), F32),
        ),
        in_specs=[hbm] * 4,
        out_specs=(hbm,) * 3,
        scratch_shapes=[
            V((16, 16, 1024), BF16), V((16, 16, 1024), BF16), V((504, 256), F32), V((1, 256), F32),
            V((501, 256), F32), pltpu.SemaphoreType.DMA((2, 4)),
        ],
        compiler_params=pltpu.CompilerParams(vmem_limit_bytes=62 * 1024 * 1024),
        name="deliver",
    )(next_keys, next_values, logits, offset)
    return next_keys, next_values, scores.T


def solution(mesh):
    in_specs = (
        P("batch", None), P("batch", None), P("batch", None),
        P("batch", "vocab", None), P("batch", "vocab", None),
        P(), P(), P(None, "batch"), P("vocab", "batch"), P("batch"),
        P(("batch", "vocab"), None), P(None, ("batch", "vocab")),
    )
    out_specs = (P("batch", "vocab", None), P("batch", "vocab", None), P(None, ("batch", "vocab")))
    return jax.shard_map(body, mesh=mesh, in_specs=in_specs, out_specs=out_specs, check_vma=False)
```

```python
import functools

import jax
import jax.numpy as jnp
from jax import lax
from jax.experimental import pallas as pl
from jax.experimental.pallas import tpu as pltpu
from jax.sharding import PartitionSpec as P

D = 8192
HEAD_DIM = 128
MESH = pl.DeviceIdType.MESH
F32 = jnp.float32
BF16 = jnp.bfloat16
NT = (((1,), (1,)), ((), ()))

BULK_EARLY_K = (2, 6)
BULK_EARLY_V = (2, 6)
BULK_BACK_K = (1, 7)
BULK_SPREAD_V = (1, 7)
BULK_MID_K = (4,)
BULK_LATE_K = (3, 5)
BULK_LATE_V = (4, 3, 5)
AWAY = (0, 1, 7, 2, 6, 3, 5, 4)


def iota(shape, axis):
    return lax.broadcasted_iota(jnp.int32, shape, axis)


def kernel(
    q_ref, kn_ref, vn_ref, kc_ref, vc_ref, par_ref, pl_ref, tl_ref, hid_ref, w_ref, gain_ref, hw_ref, past_ref,
    nk_ref, nv_ref, logit_ref, offset_ref,
    q_v, kn_v, vn_v, kc_v, vc_v, par_s, par_v, tok_v, hid_v, w_v, gain_v, hw_v, past_v,
    kt, vt, xs, xr, perm, qp, kn_s, vn_s, w_s, o_new, o_s, rs, ar, a_s, aa, ps, pr,
    ks, vs, kr, vr, nb, sq_s, sq_r, sc_s, sc_r, acc, nk_s, nv_s, lv_s, lv_r, lb_s, lb_r,
    lsem, rsem, ssem, s1, s2, t1, t2,
):
    b = lax.axis_index("batch")
    v = lax.axis_index("vocab")
    z, c = b // 2, b % 2
    kind = (c + z) % 2
    g, h = v // 2, v % 2
    x, y = v // 4, v % 4

    def same_kind(zz):
        return 2 * zz + (kind + zz) % 2

    def send(src, dst, send_sem, recv_sem, dev):
        pltpu.make_async_remote_copy(
            src_ref=src, dst_ref=dst, send_sem=send_sem, recv_sem=recv_sem,
            device_id=dev, device_id_type=MESH,
        ).start()

    def wait(ref, sem):
        pltpu.make_async_copy(ref, ref, sem).wait()

    pending = []

    def drain():
        for ref, sem in pending:
            wait(ref, sem)
        for i in list(left):
            arrived(i)

    def arrived(i):
        local[i].wait()
        left.remove(i)

    bar = pltpu.get_barrier_semaphore()

    def greet(d, _):
        pl.semaphore_signal(bar, inc=1, device_id=(b, (v + d) % 16), device_id_type=MESH)
        return 0

    def greet_batch(d, _):
        pl.semaphore_signal(bar, inc=1, device_id=((b + d) % 16, v), device_id_type=MESH)
        return 0

    def greet_pair(d, _):
        pl.semaphore_signal(
            bar, inc=1, device_id=(2 * ((z + d) % 8) + c, 2 * g + 1 - h), device_id_type=MESH
        )
        return 0

    lax.fori_loop(1, 16, greet, 0)
    lax.fori_loop(1, 16, greet_batch, 0)
    lax.fori_loop(1, 8, greet_pair, 0)

    local = [
        pltpu.make_async_copy(q_ref.at[:, pl.ds(pl.multiple_of(g * 1024, 1024), 1024)], q_v, lsem.at[0]),
        pltpu.make_async_copy(kn_ref, kn_v, lsem.at[1]),
        pltpu.make_async_copy(vn_ref, vn_v, lsem.at[2]),
        pltpu.make_async_copy(kc_ref, kc_v, lsem.at[3]),
        pltpu.make_async_copy(vc_ref, vc_v, lsem.at[4]),
        pltpu.make_async_copy(past_ref, past_v, lsem.at[5]),
        pltpu.make_async_copy(w_ref, w_v, lsem.at[6]),
        pltpu.make_async_copy(hid_ref.at[pl.ds(pl.multiple_of(v * 16, 16), 16)], hid_v, lsem.at[7]),
        pltpu.make_async_copy(hw_ref, hw_v, lsem.at[8]),
        pltpu.make_async_copy(par_ref, par_s, lsem.at[9]),
        pltpu.make_async_copy(pl_ref, par_v, lsem.at[10]),
        pltpu.make_async_copy(tl_ref, tok_v, lsem.at[11]),
        pltpu.make_async_copy(gain_ref, gain_v, lsem.at[12]),
    ]
    left = list(range(len(local)))
    for copy in local:
        copy.start()

    for i in range(3):
        arrived(i)
    lane_g = pl.ds(pl.multiple_of(g * 128, 128), 128)
    packed = jnp.concatenate(
        [q_v[...].astype(F32), kn_v[:, lane_g].astype(F32), vn_v[:, lane_g].astype(F32)], axis=1
    )
    upper = h.astype(F32)
    packed = packed[0:8] * (1.0 - upper) + packed[8:16] * upper
    packed = jnp.concatenate([packed[:, :640], packed[:, 640:]], axis=0).astype(BF16)
    xs[...] = packed
    xr[z] = packed

    pl.semaphore_wait(bar, 37)

    def send_query(d, _):
        zz = (z + d) % 8
        send(xs, xr.at[z], ssem.at[0], rsem.at[0], (same_kind(zz), v))
        return 0

    lax.fori_loop(1, 8, send_query, 0)
    pending.append((xr.at[0:7], ssem.at[0]))

    def cache_part(ref, target):
        rows = pl.ds(pl.multiple_of((target % 2) * 8, 8), 8)
        return ref.at[rows, :, pl.ds(pl.multiple_of((target // 2) * 128, 128), 128)]

    my_pos = pl.ds(pl.multiple_of(v * 16, 16), 16)

    def turn(ref, out, i):
        def step(d, _):
            t = (v + d) % 16
            send(cache_part(ref, t), out.at[:, my_pos, :], ssem.at[i], rsem.at[i], (b, t))
            return 0

        lax.fori_loop(1, 16, step, 0)
        pltpu.make_async_copy(cache_part(ref, v), out.at[:, my_pos, :], rsem.at[i]).start()

    turn(kc_ref, kt, 1)
    pending.append((kt.at[:, 0:240], ssem.at[1]))
    turn(vc_ref, vt, 2)
    pending.append((vt.at[:, 0:240], ssem.at[2]))

    for i in (3, 4, 9):
        arrived(i)

    def stage(zz, _):
        base = same_kind(zz) * 16
        count = jnp.int32(0)
        rows = [jnp.int32(0)] * 4
        for r in range(16):
            mine = (par_s[base + r] // 32 == z).astype(jnp.int32)
            for k in range(4):
                rows[k] = jnp.where(count * mine + mine == k + 1, r, rows[k])
            count = count + mine
        for k in range(4):
            ks[zz, k] = kc_v[rows[k]]
            vs[zz, k] = vc_v[rows[k]]
        return 0

    lax.fori_loop(0, 8, stage, 0)
    kr[z] = ks[z]
    vr[z] = vs[z]

    def bulk(src, dst, i, distances):
        for d in distances:
            zz = (z + d) % 8
            send(src.at[zz], dst.at[z], ssem.at[i], rsem.at[i], (same_kind(zz), v))

    bulk(ks, kr, 3, BULK_EARLY_K)
    bulk(vs, vr, 4, BULK_EARLY_V)

    lanes = iota((128, 1024), 1)
    wanted = (lanes % 128) * 8 + lanes // 128
    subs = iota((128, 1024), 0)

    def build(t, _):
        perm[pl.ds(pl.multiple_of(t * 128, 128), 128), :] = (subs + t * 128 == wanted).astype(F32).astype(BF16)
        return 0

    lax.fori_loop(0, 8, build, 0)
    k64 = iota((64, 64), 0)
    swap = (iota((64, 64), 1) == (k64 % 8) * 8 + k64 // 8).astype(F32).astype(BF16)

    for i in (5, 10, 11):
        arrived(i)
    chosen = (iota((256, 256), 0) == par_v[...]).astype(F32)
    of_parent = jnp.dot(past_v[...], chosen, precision=lax.Precision.HIGHEST, preferred_element_type=F32)
    own_token = iota((501, 256), 0) == tok_v[...] - (b * 16 + v) * 501
    acc[496:504] = jnp.zeros((8, 256), F32)
    acc[0:501] = jnp.where(own_token, of_parent, 0.0)
    picked = jnp.sum(acc[...], axis=0, keepdims=True)
    acc[496:504] = jnp.full((8, 256), -1e30, F32)

    wait(xr.at[0:7], rsem.at[0])
    got = xr[...].astype(F32)
    got = jnp.concatenate(
        [got[:, 0:8, :].reshape(64, 640), got[:, 8:16, :].reshape(64, 640)], axis=1
    ).astype(BF16)
    got = jnp.dot(swap, got, preferred_element_type=F32)
    kn_s[...] = got[:, 1024:1152]
    vn_s[...] = got[:, 1152:1280]
    qp[...] = jnp.dot(got[:, :1024].astype(BF16), perm[...], preferred_element_type=F32)
    wait(kt, rsem.at[1])
    lane256 = iota((64, 256), 1)

    def weigh(r, _):
        rows = pl.ds(pl.multiple_of(r * 8, 8), 8)
        qr = qp[rows, :]
        qf = jnp.concatenate([qr[:, j * 128:(j + 1) * 128] for j in range(8)], axis=0)
        new_key = jnp.concatenate([kn_s[rows, :]] * 8, axis=0)
        new_value = jnp.concatenate([vn_s[rows, :]] * 8, axis=0)
        s = lax.dot_general(qf.astype(BF16), kt[r], NT, preferred_element_type=F32)
        s_new = jnp.sum(qf * new_key, axis=1, keepdims=True)
        s = jnp.where(lane256 == 255, s_new, s) * HEAD_DIM ** (-0.5)
        e = jnp.exp(s - jnp.max(s, axis=1, keepdims=True))
        wf = (e / jnp.sum(e, axis=1, keepdims=True)).astype(BF16).astype(F32)
        w_s[r] = jnp.where(lane256 == 255, 0.0, wf).astype(BF16)
        o_new[r] = wf[:, 255:256] * new_value
        return 0

    lax.fori_loop(0, 8, weigh, 0, unroll=4)
    wait(vt, rsem.at[2])

    def mix(r, _):
        rows = pl.ds(pl.multiple_of(r * 8, 8), 8)
        o = jnp.dot(w_s[r], vt[r], preferred_element_type=F32) + o_new[r]
        o_s[rows, :] = jnp.concatenate([o[j * 8:(j + 1) * 8] for j in range(8)], axis=1)
        return 0

    lax.fori_loop(0, 8, mix, 0, unroll=4)
    o = lax.dot_general(o_s[...].astype(BF16), perm[...], NT, preferred_element_type=F32).astype(BF16)
    o = jnp.dot(swap, o, preferred_element_type=F32).reshape(8, 8, 1024)
    rs[...] = jnp.concatenate([o[:, :, :512], o[:, :, 512:]], axis=1).astype(BF16)
    ar[z] = rs[z]

    def send_back(d, _):
        zz = (z + d) % 8
        send(rs.at[zz], ar.at[z], ssem.at[5], rsem.at[5], (same_kind(zz), v))
        return 0

    lax.fori_loop(1, 8, send_back, 0)
    bulk(ks, kr, 3, BULK_BACK_K)
    pending.append((ar.at[0:7], ssem.at[5]))
    sub16 = iota((16, 512), 0)
    beam = jnp.zeros((16, 512), jnp.int32)
    for r in range(8):
        beam = jnp.where(sub16 % 8 == r, par_s[b * 16 + h * 8 + r] // 32, beam)
    wait(ar.at[0:7], rsem.at[5])
    att = jnp.zeros((16, 512), F32)
    for p in range(8):
        att = jnp.where(beam == p, ar[p].astype(F32), att)
    for hh in range(2):
        part = att[hh * 8:hh * 8 + 8]
        a_s[hh] = jnp.concatenate([part[:, :256], part[:, 256:]], axis=0).astype(BF16)
    aa[16 * c + 2 * z + h] = a_s[h]

    slot = aa.at[16 * c + 2 * z + h]
    send(a_s.at[1 - h], slot, ssem.at[6], rsem.at[6], (b, 2 * g + 1 - h))

    def spread(d, _):
        zz = (z + d) % 8
        for hh in range(2):
            send(a_s.at[hh], slot, ssem.at[6], rsem.at[6], (2 * zz + c, 2 * g + hh))
        return 0

    lax.fori_loop(1, 8, spread, 0)
    bulk(vs, vr, 4, BULK_SPREAD_V)
    pending.append((aa.at[0:15], ssem.at[6]))
    for i in (6, 7, 12):
        arrived(i)
    wait(aa.at[0:15], rsem.at[6])
    share = aa.at[pl.ds(16 * c, 16)]
    send(share, share, ssem.at[15], rsem.at[15], (2 * z + 1 - c, v))
    def project(core):
        rows = aa[pl.ds(16 * core, 16)].astype(F32)
        rows = jnp.concatenate(
            [rows[:, 0:8, :].reshape(128, 256), rows[:, 8:16, :].reshape(128, 256)], axis=1
        ).astype(BF16)
        part = jnp.dot(rows, w_v[...], preferred_element_type=F32).astype(BF16)
        ps[pl.ds(8 * core, 8)] = part.reshape(8, 16, 512)

        def send_partial(k, _):
            block = (v // 2 + k) % 8
            t = 2 * block + core

            @pl.when(t != v)
            def _():
                send(ps.at[8 * core + block], pr.at[v], ssem.at[7], rsem.at[7], (b, t))

            return 0

        lax.fori_loop(0, 8, send_partial, 0)

    project(c)
    wait(aa.at[0:16], rsem.at[15])
    pending.append((aa.at[0:16], ssem.at[15]))
    project(1 - c)
    pr[v] = ps[(v % 2) * 8 + v // 2]
    pending.append((pr.at[0:15], ssem.at[7]))
    bulk(ks, kr, 3, BULK_MID_K)
    wait(pr.at[0:15], rsem.at[7])
    residual = hid_v[...].astype(F32) + jnp.sum(pr[...].astype(F32), axis=0)
    nb[c, v, 0] = (residual * gain_v[...]).astype(BF16)

    for slot in (1, 2, 3, 4, 5, 6, 7):
        zz = (z - AWAY[slot]) % 8
        send(nb.at[c, v, 0], nb.at[c, v, slot], ssem.at[8], rsem.at[8 if slot < 5 else 14], (2 * zz + c, v))
    pending.append((nb.at[0, 0, 0:7], ssem.at[8]))

    def send_own(d, _):
        send(nb.at[c, v, 0], nb.at[c, v, 0], ssem.at[10], rsem.at[16], (b, (v + d) % 16))
        return 0

    lax.fori_loop(1, 16, send_own, 0)
    lane256 = iota((16, 256), 1)
    square = jnp.sum(residual * residual, axis=1, keepdims=True)
    square = jnp.where(lane256 == iota((16, 256), 0) + 16 * v, square, 0.0)
    square = jnp.sum(square, axis=0, keepdims=True)
    sq_s[...] = square
    sq_r[b] = square

    def send_square(d, _):
        send(sq_s, sq_r.at[b], ssem.at[9], rsem.at[9], ((b + d) % 16, v))
        return 0

    lax.fori_loop(1, 16, send_square, 0)
    pending.append((sq_r.at[0:15], ssem.at[9]))

    def along(u, axis, d):
        if axis == 0:
            return ((u // 4 + d) % 4) * 4 + u % 4
        return (u // 4) * 4 + (u % 4 + d) % 4

    def piece(u, half, part=None):
        start, size = ((1, 4), (5, 3))[half]
        if part == 0:
            size = 2
        elif part == 1:
            start, size = start + 2, size - 2
        return nb.at[c, u, start:start + size]

    def state(ref, axis, d, sem):
        send(ref, ref, ssem.at[10], sem, (b, along(v, axis, d)))

    def sibling(ref, i=10):
        send(ref, ref, ssem.at[11], rsem.at[i], (2 * z + 1 - c, v))

    halves = ((1, 0), (0, 1))

    def first(half, order=halves):
        axis = order[half][0]
        state(piece(v, half), axis, 1, s1.at[half, 0])
        state(piece(v, half), axis, -1, s1.at[half, 1])
        state(piece(v, half), axis, 2, s2.at[half])

    def second(half, o):
        u = along(v, halves[half][0], o)
        axis = halves[half][1]
        state(piece(u, half), axis, 1, t1.at[half, o, 0])
        state(piece(u, half), axis, -1, t1.at[half, o, 1])
        if o == 2:
            state(piece(u, half), axis, 2, t2.at[half, o, 0])

    def second_forward(half, o):
        u = along(v, halves[half][0], o)
        axis = halves[half][1]
        wait(piece(u, half), t1.at[half, o, 0])
        state(piece(along(u, axis, -1), half, 0), axis, 1, t2.at[half, o, 0])
        sibling(piece(along(u, axis, -1), half))
        wait(piece(u, half), t1.at[half, o, 1])
        state(piece(along(u, axis, 1), half, 1), axis, -1, t2.at[half, o, 1])
        sibling(piece(along(u, axis, 1), half))

    for half in range(2):
        if half == 0:
            wait(nb.at[0, 0, 0:4], rsem.at[8])
        else:
            wait(nb.at[0, 0, 0:3], rsem.at[14])
        first(half)
        second(half, 0)
        sibling(piece(v, half))
    bulk(vs, vr, 4, BULK_LATE_V)
    bulk(ks, kr, 3, BULK_LATE_K)
    wait(nb.at[0, 0:15, 0], rsem.at[16])
    sibling(nb.at[c, :, 0], 17)
    for half in range(2):
        wait(piece(v, half), s1.at[half, 0])
        second(half, 3)
        wait(piece(v, half), s1.at[half, 1])
        second(half, 1)
        sibling(piece(along(v, halves[half][0], -1), half))
        sibling(piece(along(v, halves[half][0], 1), half))
    for half in range(2):
        second_forward(half, 0)
    for half in range(2):
        wait(piece(v, half), s2.at[half])
        second(half, 2)
        sibling(piece(along(v, halves[half][0], 2), half))

    wait(sq_r.at[0:15], rsem.at[9])
    scale = lax.rsqrt(jnp.sum(sq_r[...], axis=0) / D + 1e-05)
    scale = jnp.where(iota((1, 256), 1) // 16 == v, scale, 0.0)
    sc_s[...] = scale
    sc_r[v] = scale

    def send_scale(d, _):
        send(sc_s, sc_r.at[v], ssem.at[12], rsem.at[11], (b, (v + d) % 16))
        return 0

    lax.fori_loop(1, 16, send_scale, 0)
    pending.append((sc_r.at[0:15], ssem.at[12]))
    for o in (3, 1):
        for half in range(2):
            second_forward(half, o)
    arrived(8)

    def product(core, slot):
        away = jnp.where(slot % 2 == 1, (slot + 1) // 2, (8 - slot // 2) % 8)
        cols = pl.ds(pl.multiple_of((2 * ((z + away) % 8) + core) * 512, 512), 512)
        return lax.dot_general(
            hw_v[:, cols], nb[core, :, slot].reshape(256, 512), NT, preferred_element_type=F32
        )

    acc[0:501] = product(c, 0)
    wait(nb.at[0, :, 0], rsem.at[17])
    acc[0:501] += product(1 - c, 0)
    for o in (0, 3, 1, 2):
        for half in range(2):
            u = along(v, halves[half][0], o)
            axis = halves[half][1]
            if o == 2:
                for k in range(2):
                    wait(piece(u, half), t1.at[half, o, k])
                    sibling(piece(along(u, axis, 2 * k - 1), half))
                wait(piece(u, half), t2.at[half, o, 0])
            else:
                wait(piece(u, half, 0), t2.at[half, o, 0])
                wait(piece(u, half, 1), t2.at[half, o, 1])
            sibling(piece(along(u, axis, 2), half))

    pending.append((nb.at[0, 0:15], ssem.at[10]))
    pending.append((nb.at[0], ssem.at[11]))

    def several(core, first_slot, count):
        return sum(product(core, first_slot + k) for k in range(1, count)) + product(core, first_slot)

    acc[0:501] += several(c, 1, 4)
    acc[0:501] += several(c, 5, 3)
    wait(nb.at[0, 0:14], rsem.at[10])

    acc[0:501] += several(1 - c, 1, 4)
    acc[0:501] += several(1 - c, 5, 3)
    wait(sc_r.at[0:15], rsem.at[11])
    logits = acc[...] * jnp.sum(sc_r[...], axis=0)
    acc[...] = logits
    results = [
        pltpu.make_async_copy(acc, logit_ref, lsem.at[15]),
        pltpu.make_async_copy(nk_s, nk_ref, lsem.at[13]),
        pltpu.make_async_copy(nv_s, nv_ref, lsem.at[14]),
    ]
    results[0].start()
    largest = jnp.max(logits, axis=0, keepdims=True)
    total = jnp.sum(jnp.exp(logits - largest), axis=0, keepdims=True)

    def merged(stats):
        high = jnp.max(stats[:, 0:1], axis=0)
        total = jnp.sum(stats[:, 1:2] * jnp.exp(stats[:, 0:1] - high), axis=0)
        return jnp.concatenate([high, total, jnp.sum(stats[:, 2:4], axis=0)], axis=0)

    stats = jnp.concatenate([largest, total, picked, jnp.zeros((1, 256), F32)], axis=0)
    lv_s[...] = stats
    lv_r[v] = stats

    def send_vocab(d, _):
        send(lv_s, lv_r.at[v], ssem.at[13], rsem.at[12], (b, (v + d) % 16))
        return 0

    lax.fori_loop(1, 16, send_vocab, 0)
    pending.append((lv_r.at[0:15], ssem.at[13]))
    wait(lv_r.at[0:15], rsem.at[12])
    stats = merged(lv_r[...])
    lb_s[...] = stats
    lb_r[b] = stats

    def send_batch(d, _):
        send(lb_s, lb_r.at[b], ssem.at[14], rsem.at[13], ((b + d) % 16, v))
        return 0

    lax.fori_loop(1, 16, send_batch, 0)
    pending.append((lb_r.at[0:15], ssem.at[14]))

    wait(kr.at[0:7], rsem.at[3])
    wait(vr.at[0:7], rsem.at[4])
    last = iota((16, 1024), 0) == jnp.where(v == 15, 15, 99)
    new_keys = kn_v[...].astype(F32)
    new_values = vn_v[...].astype(F32)
    beams = [par_s[b * 16 + r] // 32 for r in range(16)]
    for r in range(16):
        at = jnp.int32(0)
        for earlier in range(r):
            at = at + (beams[earlier] == beams[r]).astype(jnp.int32)
        at = jnp.minimum(at, 3)
        nk_s[r] = jnp.where(last, new_keys[r:r + 1], kr[beams[r], at].astype(F32)).astype(BF16)
        nv_s[r] = jnp.where(last, new_values[r:r + 1], vr[beams[r], at].astype(F32)).astype(BF16)

    for copy in results[1:]:
        copy.start()
    wait(lb_r.at[0:15], rsem.at[13])
    stats = merged(lb_r[...])
    offset_ref[...] = stats[2:3] - (stats[0:1] + jnp.log(stats[1:2]))

    for copy in results:
        copy.wait()
    pending.append((kr.at[0:7], ssem.at[3]))
    pending.append((vr.at[0:7], ssem.at[4]))
    drain()


def deliver(nk_in, nv_in, logit_in, offset_in, nk_out, nv_out, cand_out, nk_v, nv_v, logit_v, offset_v, cand_v, sem):
    loads = [
        pltpu.make_async_copy(src, held, sem.at[0, i])
        for i, (src, held) in enumerate(((logit_in, logit_v), (nk_in, nk_v), (nv_in, nv_v), (offset_in, offset_v)))
    ]
    stores = [
        pltpu.make_async_copy(held, dst, sem.at[1, i])
        for i, (held, dst) in enumerate(((cand_v, cand_out), (nk_v, nk_out), (nv_v, nv_out)))
    ]
    for load in loads:
        load.start()
    for i in (1, 2, 0):
        loads[i].wait()
        if i == 0:
            loads[3].wait()
            cand_v[...] = logit_v[0:501] + offset_v[...]
        stores[i].start()
    for store in stores:
        store.wait()


def body(
    queries, key_new, value_new, key_cache, value_cache, parents, tokens, hidden, out_weight, final_gain,
    head_weight, past_scores,
):
    hbm = pl.BlockSpec(memory_space=pltpu.HBM)
    vmem = pl.BlockSpec(memory_space=pltpu.VMEM)
    V = pltpu.VMEM
    scratch = [
        V((16, 1024), BF16), V((16, 1024), BF16), V((16, 1024), BF16),
        V((16, 16, 1024), BF16), V((16, 16, 1024), BF16),
        pltpu.SMEM((256,), jnp.int32), V((1, 256), jnp.int32), V((1, 256), jnp.int32),
        V((16, 512), BF16), V((512, 512), BF16), V((1, 512), F32),
        V((501, 8192), BF16), V((501, 256), F32),
        V((8, 256, 128), BF16), V((8, 256, 128), BF16),
        V((16, 640), BF16), V((8, 16, 640), BF16), V((1024, 1024), BF16),
        V((64, 1024), F32), V((64, 128), F32), V((64, 128), F32),
        V((8, 64, 256), BF16), V((8, 64, 128), F32), V((64, 1024), F32),
        V((8, 16, 512), BF16), V((8, 16, 512), BF16),
        V((2, 16, 256), BF16), V((32, 16, 256), BF16),
        V((16, 16, 512), BF16), V((16, 16, 512), BF16),
        V((8, 4, 16, 1024), BF16), V((8, 4, 16, 1024), BF16),
        V((8, 4, 16, 1024), BF16), V((8, 4, 16, 1024), BF16),
        V((2, 16, 8, 16, 512), BF16),
        V((1, 256), F32), V((16, 1, 256), F32), V((1, 256), F32), V((16, 1, 256), F32),
        V((504, 256), F32), V((16, 16, 1024), BF16), V((16, 16, 1024), BF16),
        V((4, 256), F32), V((16, 4, 256), F32), V((4, 256), F32), V((16, 4, 256), F32),
        pltpu.SemaphoreType.DMA((16,)), pltpu.SemaphoreType.DMA((18,)), pltpu.SemaphoreType.DMA((16,)),
        pltpu.SemaphoreType.DMA((2, 2)), pltpu.SemaphoreType.DMA((2,)),
        pltpu.SemaphoreType.DMA((2, 4, 2)), pltpu.SemaphoreType.DMA((2, 4, 2)),
    ]
    next_keys, next_values, logits, offset = pl.pallas_call(
        kernel,
        out_shape=(
            jax.ShapeDtypeStruct((16, 16, 1024), BF16),
            jax.ShapeDtypeStruct((16, 16, 1024), BF16),
            jax.ShapeDtypeStruct((504, 256), F32),
            jax.ShapeDtypeStruct((1, 256), F32),
        ),
        in_specs=[hbm] * 13,
        out_specs=(hbm, hbm, hbm, vmem),
        scratch_shapes=scratch,
        compiler_params=pltpu.CompilerParams(
            collective_id=0, has_side_effects=True, vmem_limit_bytes=62 * 1024 * 1024
        ),
        name="beam_step",
    )(
        queries, key_new, value_new, key_cache, value_cache, parents, parents.reshape(1, 256), tokens.reshape(1, 256),
        hidden, out_weight, final_gain.reshape(1, 512), head_weight, past_scores.T,
    )
    next_keys, next_values, scores = pl.pallas_call(
        deliver,
        out_shape=(
            jax.ShapeDtypeStruct((16, 16, 1024), BF16),
            jax.ShapeDtypeStruct((16, 16, 1024), BF16),
            jax.ShapeDtypeStruct((501, 256), F32),
        ),
        in_specs=[hbm] * 4,
        out_specs=(hbm,) * 3,
        scratch_shapes=[
            V((16, 16, 1024), BF16), V((16, 16, 1024), BF16), V((504, 256), F32), V((1, 256), F32),
            V((501, 256), F32), pltpu.SemaphoreType.DMA((2, 4)),
        ],
        compiler_params=pltpu.CompilerParams(vmem_limit_bytes=62 * 1024 * 1024),
        name="deliver",
    )(next_keys, next_values, logits, offset)
    return next_keys, next_values, scores.T


def solution(mesh):
    in_specs = (
        P("batch", None), P("batch", None), P("batch", None),
        P("batch", "vocab", None), P("batch", "vocab", None),
        P(), P(), P(None, "batch"), P("vocab", "batch"), P("batch"),
        P(("batch", "vocab"), None), P(None, ("batch", "vocab")),
    )
    out_specs = (P("batch", "vocab", None), P("batch", "vocab", None), P(None, ("batch", "vocab")))
    return jax.shard_map(body, mesh=mesh, in_specs=in_specs, out_specs=out_specs, check_vma=False)
```
